128 devices in a mesh: ens: 4 (over x), sp: 32 (over y, z, core).
Axes of the slice: x: 4, y: 4, z: 4, core: 2. Of those that a mesh axis runs over, the one named last changes fastest.
Arguments:
- latent: bfloat16 [8, 32768, 1024], P('ens', 'sp'), may hold values from -6 to 6
- w_in: bfloat16 [1024, 1024], replicated, may hold values from -0.1875 to 0.1875
- output_weight: bfloat16 [80, 1024], replicated, may hold values from -0.1875 to 0.1875
- targets: bfloat16 [80, 32768], P(None, 'sp'), may hold values from -6 to 6
- area_weights: float32 [32768], P('sp'), may hold values from 1 to 300, as said below
- live_counts: int32 [32], P('sp'), may hold values from 1 to 1024, 28672 in all
Outputs:
- loss: float32 [], replicated
- grad_latent: bfloat16 [8, 32768, 1024], P('ens', 'sp')
- grad_w_in: float32 [1024, 1024], P('sp')
- grad_w_out: float32 [80, 1024], replicated
The draws below stay inside these ranges and needn't reach their ends.
Inputs may be any that keep to these rules, and one draw needn't show every extreme that they name: `area_weights`: weights of one block of 1024 points share a factor that differs between blocks. `live_counts`: each entry counts the owned points at the start of one block of 1024; some entry equals 1024.
All inputs are finite; a program needn't handle non-finite values.
Results may differ from the reference program's by a relative error of at most 0.0095.
Values may be sent and summed in bfloat16 or wider, within the bound.
A program may use at most 128 MiB of HBM per device.

```python
import math
import jax
import jax.numpy as jnp
import numpy as np
from jax import lax

H = 1024
V = 80
PTS_DEV = 1024
MEMBERS = 8
POINTS = 32768
N_SP = 32


def draw_latent(key, part):
    key = jax.random.fold_in(key, 5)
    base = jnp.clip(jax.random.normal(key, (MEMBERS, POINTS, H), jnp.float32), -6.0, 6.0)
    within = (jnp.arange(POINTS) % PTS_DEV).astype(jnp.float32) / max(PTS_DEV - 1, 1)
    rising = (jnp.arange(MEMBERS) >= 2).astype(jnp.float32)
    factor = 1.0 + rising[:, None] * (within[None, :] - 0.4)
    return jnp.clip(base * factor[:, :, None], -6.0, 6.0).astype(jnp.bfloat16)


def draw_area_weights(key, part):
    key = jax.random.fold_in(key, 7)
    point_key, block_key = jax.random.split(key, 2)
    blocks = POINTS // PTS_DEV
    point_part = jax.random.uniform(point_key, (POINTS,), jnp.float32)
    block_part = jax.random.uniform(block_key, (blocks,), jnp.float32)
    block_factor = jnp.exp(math.log(30.0) * block_part)
    return jnp.power(10.0, point_part) * jnp.repeat(block_factor, PTS_DEV)


def levels(own_key, shape, cuts, smallest, largest):
    gain = 1.0
    for dim, parts in cuts:
        draws = jax.random.uniform(jax.random.fold_in(jax.random.fold_in(own_key, 6), dim), (parts,), jnp.float32, smallest / len(cuts), largest / len(cuts))
        gain = gain * jnp.repeat(jnp.exp(draws), shape[dim] // parts).reshape((-1,) + (1,) * (len(shape) - 1 - dim))
    return gain


def profile(count, total, bound, slope):
    weights = [(1 << 20) // math.isqrt(standing ** slope) + 1 for standing in range(2, count + 1)]
    spare, given = total - bound - (count - 1), [1] * (count - 1)
    while spare > 0:
        movable = [i for i in range(count - 1) if given[i] < bound]
        whole, remaining = sum([weights[i] for i in movable]), spare
        for i in movable:
            addition = min(bound - given[i], max(1, remaining * weights[i] // whole), spare)
            given[i] = given[i] + addition
            spare = spare - addition
    return np.array([bound] + given)


def uneven(key, amount, total, most, skew):
    if amount == 2:
        one = jax.random.randint(key, (), max(1, total - most), min(most, total - 1) + 1)
        return jnp.stack([one, total - one])
    lengths = jnp.asarray(profile(amount, total, most, skew), jnp.int32)
    pairs = (amount - 1) // 2
    giver, receiver = lengths[1:1 + 2 * pairs:2], lengths[2:2 + 2 * pairs:2]
    margin = jnp.minimum(giver - 1, most - receiver)
    shifted = jax.random.randint(jax.random.fold_in(key, 1), (pairs,), 0, 1 << 20) % (margin + 1)
    lengths = lengths.at[1:1 + 2 * pairs:2].set(giver - shifted).at[2:2 + 2 * pairs:2].set(receiver + shifted)
    return lengths[jax.random.permutation(jax.random.fold_in(key, 2), amount)]


def normal_values(own_key, extent, deviation, most, cuts=(), held_as=jnp.bfloat16):
    array = jax.random.normal(own_key, extent, jnp.float32) * deviation
    if len(cuts) > 0:
        array = levels(own_key, extent, cuts, -0.22, 0.18) * array
    return jnp.clip(array, min=-most, max=most).astype(held_as)


def setup_inputs(seed: int = 0) -> dict:
    streams_of = jax.random.split(jax.random.key(seed), 7)
    latent = draw_latent(jax.random.fold_in(streams_of[6], 71), 0)
    w_in = normal_values(streams_of[1], (H, H), H ** -0.5, 0.1875)
    output_weight = normal_values(streams_of[2], (V, H), H ** -0.5, 0.1875)
    targets = normal_values(streams_of[3], (V, POINTS), 1.0, 6.0, ((1, 32),))
    area_weights = draw_area_weights(jax.random.fold_in(streams_of[6], 71), 0)
    live_counts = uneven(streams_of[5], N_SP, PTS_DEV * N_SP * 7 // 8, PTS_DEV, 1).astype(jnp.int32)
    return dict(latent=latent, w_in=w_in, output_weight=output_weight, targets=targets, area_weights=area_weights, live_counts=live_counts)


loss_scale = 1024.0
smoothing = 1.0

def partial_skill_terms(members, measured_target_slice, kernel_softening_widths):
    n_members = members.shape[0]
    diff_obs = members - measured_target_slice[None]
    obs_norm = jnp.sqrt(lax.optimization_barrier(jnp.sum(diff_obs * diff_obs, axis=1)) + smoothing)
    pair_diff = members[:, None] - members[None, :]
    pair_norm = jnp.sqrt(lax.optimization_barrier(jnp.sum(pair_diff * pair_diff, axis=2)) + smoothing)
    spread = lax.optimization_barrier(jnp.sum(pair_norm, axis=(0, 1))) - n_members * 1.0
    ensemble_skill_values = lax.optimization_barrier(jnp.sum(obs_norm, axis=0)) / n_members - spread / (2.0 * n_members * (n_members - 1))
    derivative_coefficients = diff_obs / (n_members * obs_norm[:, None]) - lax.optimization_barrier(jnp.sum(pair_diff / pair_norm[:, :, None], axis=1)) / (n_members * (n_members - 1))
    return (ensemble_skill_values, derivative_coefficients * kernel_softening_widths[None, None])

def reference(latent, w_in, output_weight, targets, area_weights, live_counts):
    n_members, points, feature_width = latent.shape
    shards = live_counts.shape[0]
    per_shard = points // shards
    position = jnp.arange(points, dtype=jnp.int32)
    is_live = (position % per_shard < live_counts[position // per_shard]).astype(jnp.float32)
    weighted = area_weights * is_live
    weight_total = jnp.sum(weighted)
    live_total = jnp.sum(is_live)
    scales_all = loss_scale * live_total * weighted / weight_total
    w_in_f = w_in.astype(jnp.float32)
    decoder_matrix_single_precision = output_weight.astype(jnp.float32)

    def one_shard(totals, shard_index):
        offset = (shard_index * per_shard).astype(jnp.int32)
        latent_block = lax.dynamic_slice_in_dim(latent, offset, per_shard, 1).astype(jnp.float32)
        measured_target_slice = lax.dynamic_slice_in_dim(targets, offset, per_shard, 1).astype(jnp.float32)
        kernel_softening_widths = lax.dynamic_slice_in_dim(scales_all, offset, per_shard, 0)
        weight_block = lax.dynamic_slice_in_dim(weighted, offset, per_shard, 0)
        pre_act = jnp.einsum('mph,hk->mpk', latent_block, w_in_f)
        latent_activations = lax.optimization_barrier(jax.nn.gelu(pre_act).astype(jnp.bfloat16)).astype(jnp.float32)
        ensemble_prediction = jnp.einsum('mp,hjp->hmj', decoder_matrix_single_precision, latent_activations)
        ensemble_prediction = lax.optimization_barrier(ensemble_prediction.astype(jnp.bfloat16)).astype(jnp.float32)
        ensemble_skill_values, derivative_coefficients = partial_skill_terms(ensemble_prediction, measured_target_slice, kernel_softening_widths)
        derivative_coefficients = lax.optimization_barrier(derivative_coefficients.astype(jnp.bfloat16)).astype(jnp.float32)
        back_hidden = jnp.einsum('vk,mvp->mpk', decoder_matrix_single_precision, derivative_coefficients)
        unused_out, gelu_pull = jax.vjp(jax.nn.gelu, pre_act)
        back_pre = lax.optimization_barrier(gelu_pull(back_hidden)[0].astype(jnp.bfloat16)).astype(jnp.float32)
        grad_block = jnp.einsum('mpk,hk->mph', back_pre, w_in_f).astype(jnp.bfloat16)
        sum_in = totals[0] + jnp.einsum('mph,mpk->hk', latent_block, back_pre)
        sum_out = totals[1] + jnp.einsum('mvp,mpk->vk', derivative_coefficients, latent_activations)
        sum_loss = totals[2] + jnp.sum(weight_block * ensemble_skill_values)
        return ((sum_in, sum_out, sum_loss), grad_block)
    init = (jnp.zeros((feature_width, feature_width), jnp.float32), jnp.zeros(output_weight.shape, jnp.float32), jnp.zeros((), jnp.float32))
    totals, grad_blocks = lax.scan(one_shard, init, jnp.arange(shards, dtype=jnp.int32))
    grad_latent = jnp.moveaxis(grad_blocks, 0, 1).reshape(n_members, points, feature_width)
    return (totals[2] / weight_total, grad_latent, totals[0] / live_total, totals[1] / live_total)
```

```python
import functools
import math

import jax
import jax.numpy as jnp
from jax import lax
from jax.experimental import pallas as pl
from jax.experimental.pallas import tpu as pltpu
from jax.sharding import PartitionSpec as P

BF16, F32 = jnp.bfloat16, jnp.float32
MESH = pl.DeviceIdType.MESH
LOSS_SCALE = 1024.0
MEMBERS, VARS, FEATURES, POINTS = 8, 80, 1024, 1024
CHUNKS = 2
CHUNK = POINTS // CHUNKS
LANES = 128
PIECES = 2
WIDE = FEATURES // PIECES
ROWS = 32
OUTER = math.sqrt(2.0 / math.pi)
INNER = OUTER * 0.044715


def dot(a, b, ca, cb):
    return lax.dot_general(a, b, (((ca,), (cb,)), ((), ())), preferred_element_type=F32)


def activation(z):
    cubic = INNER * (z * z)
    s = 0.5 * jnp.tanh(z * (cubic + OUTER)) + 0.5
    h = z * s
    slope = s + (h - h * s) * (6.0 * cubic + 2.0 * OUTER)
    return h.astype(BF16), slope.astype(BF16)


def score_block(x_ref, y, weighted, scales, store):
    n = MEMBERS
    pairs = [(i, j) for i in range(n) for j in range(i + 1, n)]
    step = 16
    own = [jnp.zeros((step, LANES), F32) for _ in range(n)]
    between = [jnp.zeros((step, LANES), F32) for _ in pairs]
    for v in range(0, VARS, step):
        x = [x_ref[m // 2, m % 2, v : v + step, :].astype(F32) for m in range(n)]
        for m in range(n):
            d = x[m] - y[v : v + step]
            own[m] = own[m] + d * d
        for q, (i, j) in enumerate(pairs):
            d = x[i] - x[j]
            between[q] = between[q] + d * d
    a = [jnp.sqrt(jnp.sum(o, axis=0, keepdims=True) + 1.0) for o in own]
    b = [jnp.sqrt(jnp.sum(o, axis=0, keepdims=True) + 1.0) for o in between]
    score = sum(a) / n - sum(b) / (n * (n - 1.0))
    from_target = [scales / (n * t) for t in a]
    from_pair = [scales / (n * (n - 1.0) * t) for t in b]
    for v in range(0, VARS, step):
        x = [x_ref[m // 2, m % 2, v : v + step, :].astype(F32) for m in range(n)]
        total = [(x[m] - y[v : v + step]) * from_target[m] for m in range(n)]
        for q, (i, j) in enumerate(pairs):
            d = (x[i] - x[j]) * from_pair[q]
            total[i] = total[i] - d
            total[j] = total[j] + d
        for m in range(n):
            store(m, v, step, total[m].astype(BF16))
    return weighted * score


def kernel(
    lat_hbm, w_hbm, wout, targets, area, live,
    loss_out, glat_hbm, gwin_out, gwout_out,
    lat, w, hid, back, acc, fsend, frecv, ssend, srecv, gout, gparts,
    core_send, core_recv, one_send, one_recv, two_send, two_recv, three,
    g_core_send, g_core_recv, g_y_send, g_y_recv, g_z, g_x, g_all,
    wt_core, wt_z, wt_y, ls_core, ls_y, ls_z, ls_x,
    in_sem, out_sem, f_ss, f_rs, s_ss, s_rs, p_ss, p_rs, g_ss, g_rs, t_ss, t_rs,
):
    e = lax.axis_index("ens")
    sp = lax.axis_index("sp")
    core = lax.rem(sp, 2)
    z = lax.rem(sp // 2, 4)
    y = sp // 8

    def turn(i, d):
        return lax.rem(i + d, 4)

    def device(x_, y_, z_, core_):
        return (x_, (y_ * 4 + z_) * 2 + core_)

    along = {
        "x": lambda d: device(turn(e, d), y, z, core),
        "y": lambda d: device(e, turn(y, d), z, core),
        "z": lambda d: device(e, y, turn(z, d), core),
    }
    place = {"x": e, "y": y, "z": z}
    sibling = device(e, y, z, 1 - core)

    def load(m, c):
        s = pl.ds(c * CHUNK, CHUNK)
        return pltpu.make_async_copy(lat_hbm.at[m, s], lat.at[m, s], in_sem.at[1 + 2 * c + m])

    load_w = pltpu.make_async_copy(w_hbm, w, in_sem.at[0])
    load_w.start()
    loads = {(c, m): load(m, c) for c in range(CHUNKS) for m in range(2)}
    for cp in loads.values():
        cp.start()

    peers = [along[k](d) for k in "xyz" for d in (1, 2, 3)] + [sibling]
    peers += [device(e, turn(y, d), z, 1 - core) for d in (1, 2, 3)]
    barrier = pltpu.get_barrier_semaphore()
    for p in peers:
        pl.semaphore_signal(barrier, inc=1, device_id=p, device_id_type=MESH)

    def send(src, dst, ss, rs, to):
        cp = pltpu.make_async_remote_copy(
            src_ref=src, dst_ref=dst, send_sem=ss, recv_sem=rs, device_id=to, device_id_type=MESH
        )
        cp.start()
        return cp

    started = []

    def spread(axis, src, dst, ss, rs):
        cps = []
        for d in (2, 1, 3):
            cps.append(send(src(turn(place[axis], d)), dst(d, place[axis]), ss.at[d - 1], rs.at[d - 1], along[axis](d)))
        started.extend(cps)
        return cps

    def arrive(cps):
        for cp in cps:
            cp.wait_recv()

    where = lax.broadcasted_iota(jnp.int32, (8, LANES), 0) * LANES + lax.broadcasted_iota(jnp.int32, (8, LANES), 1)
    is_live = (where < live[0]).astype(F32)
    weighted_all = area[...] * is_live
    first = lax.broadcasted_iota(jnp.int32, (8, LANES), 0) == 0
    wt_own = jnp.where(
        first, jnp.sum(weighted_all, axis=0, keepdims=True), jnp.sum(is_live, axis=0, keepdims=True)
    )
    wt_core[core] = wt_own

    def forward(c, m):
        loads[c, m].wait()
        s = pl.ds(c * CHUNK, CHUNK)
        pre = jnp.dot(lat[m, s, :], w[...], preferred_element_type=F32)
        h, g = activation(pre)
        hid[m, s, :] = h
        back[m, s, :] = g
        f = dot(wout[...], hid[m, s, :], 1, 1).astype(BF16)
        for k in range(4):
            fsend[c, k, m] = f[:, k * LANES : (k + 1) * LANES]
        frecv[c, e, m] = fsend[c, e, m]

    def forward_send(c, m):
        return spread(
            "x", lambda k: fsend.at[c, k, m], lambda d, own: frecv.at[c, own, m], f_ss.at[c, m], f_rs.at[c, m]
        )

    loss_rows = []

    def scored(c):
        block = c * 4 + e
        y_block = targets[:, pl.ds(pl.multiple_of(block * LANES, LANES), LANES)].astype(F32)
        lanes = lax.broadcasted_iota(jnp.int32, (1, LANES), 1)
        weighted = area[pl.ds(block, 1), :] * (block * LANES + lanes < live[0]).astype(F32)
        scales = LOSS_SCALE * live_total * weighted / weight_total

        def store(m, v, step, value):
            ssend[c, m // 2, m % 2, v : v + step, :] = value

        loss_rows.append(score_block(frecv.at[c], y_block, weighted, scales, store))
        srecv[c, e] = ssend[c, e]
        return spread("x", lambda k: ssend.at[c, k], lambda d, own: srecv.at[c, own], s_ss.at[c], s_rs.at[c])

    load_w.wait()
    forward(0, 0)
    pl.semaphore_wait(barrier, len(peers))
    f00 = forward_send(0, 0)
    tw = send(wt_core.at[core], wt_core.at[core], t_ss.at[0], t_rs.at[0], sibling)
    started.append(tw)
    forward(0, 1)
    f01 = forward_send(0, 1)
    arrive([tw])
    wt_z[z] = wt_core[0] + wt_core[1]
    tw = spread("z", lambda k: wt_z.at[z], lambda d, own: wt_z.at[own], t_ss.at[pl.ds(1, 3)], t_rs.at[pl.ds(1, 3)])
    forward(1, 0)
    f10 = forward_send(1, 0)
    arrive(tw)
    wt_y[y] = (wt_z[0] + wt_z[1]) + (wt_z[2] + wt_z[3])
    tw = spread("y", lambda k: wt_y.at[y], lambda d, own: wt_y.at[own], t_ss.at[pl.ds(4, 3)], t_rs.at[pl.ds(4, 3)])
    forward(1, 1)
    f11 = forward_send(1, 1)
    arrive(tw)
    totals = jnp.sum((wt_y[0] + wt_y[1]) + (wt_y[2] + wt_y[3]), axis=1, keepdims=True)
    weight_total = totals[0:1, 0:1]
    live_total = totals[1:2, 0:1]

    arrive(f00)
    arrive(f01)
    s0 = scored(0)
    arrive(f10)
    arrive(f11)
    s1 = scored(1)

    def backward(c):
        s = pl.ds(c * CHUNK, CHUNK)
        for m in range(2):
            slopes = jnp.concatenate([srecv[c, k, m] for k in range(4)], axis=1)
            bh = dot(slopes, wout[...], 0, 0)
            back[m, s, :] = (back[m, s, :].astype(F32) * bh).astype(BF16)
            part = dot(slopes, hid[m, s, :], 1, 0)
            if c == 0 and m == 0:
                gout[...] = part
            else:
                gout[...] += part

    def weight_piece(c, j):
        s = pl.ds(c * CHUNK, CHUNK)
        cols = slice(j * WIDE, (j + 1) * WIDE)
        a = lat[:, s, :].reshape(2 * CHUNK, FEATURES)
        b = back[:, s, cols].reshape(2 * CHUNK, WIDE)
        return dot(a, b, 0, 0).reshape(2 * 16, ROWS, WIDE)

    arrive(s0)
    backward(0)
    for j in range(PIECES):
        acc[j] = weight_piece(0, j)

    loss_tile = jnp.broadcast_to(loss_rows[0] + loss_rows[1], (8, LANES))
    ls_core[core] = loss_tile
    lc = send(ls_core.at[core], ls_core.at[core], t_ss.at[7], t_rs.at[7], sibling)
    started.append(lc)

    arrive(s1)
    backward(1)

    def g_start():
        def body(k, _):
            cols = pl.ds(pl.multiple_of((k * 2 + 1 - core) * LANES, LANES), LANES)
            g_core_send[k] = gout[:, cols].astype(BF16)
            return 0

        lax.fori_loop(0, 4, body, 0)
        cp = send(g_core_send, g_core_recv, g_ss.at[0], g_rs.at[0], sibling)
        started.append(cp)
        return [cp]

    def g_to_y(cps):
        arrive(cps)

        def body(k, _):
            cols = pl.ds(pl.multiple_of((k * 2 + core) * LANES, LANES), LANES)
            g_y_send[k] = (gout[:, cols] + g_core_recv[k].astype(F32)).astype(BF16)
            return 0

        lax.fori_loop(0, 4, body, 0)
        return spread(
            "y", lambda k: g_y_send.at[k], lambda d, own: g_y_recv.at[d - 1], g_ss.at[pl.ds(1, 3)], g_rs.at[pl.ds(1, 3)]
        )

    def g_to_z(cps):
        arrive(cps)
        total = g_y_send[y].astype(F32)
        for d in range(3):
            total = total + g_y_recv[d].astype(F32)
        g_z[z] = total.astype(BF16)
        return spread(
            "z", lambda k: g_z.at[z], lambda d, own: g_z.at[own], g_ss.at[pl.ds(4, 3)], g_rs.at[pl.ds(4, 3)]
        )

    def four(ref):
        return (ref[0].astype(F32) + ref[1].astype(F32)) + (ref[2].astype(F32) + ref[3].astype(F32))

    def g_to_x(cps):
        arrive(cps)
        g_x[e] = four(g_z).astype(BF16)
        return spread(
            "x", lambda k: g_x.at[e], lambda d, own: g_x.at[own], g_ss.at[pl.ds(7, 3)], g_rs.at[pl.ds(7, 3)]
        )

    def g_to_all(cps):
        arrive(cps)
        mine = y * 2 + core
        g_all[mine] = four(g_x) / live_total
        out = [send(g_all.at[mine], g_all.at[mine], g_ss.at[10], g_rs.at[10], sibling)]
        for d in (1, 2, 3):
            out.append(send(g_all.at[mine], g_all.at[mine], g_ss.at[10 + d], g_rs.at[10 + d], along["y"](d)))
        for d in (1, 2, 3):
            to = device(e, turn(y, d), z, 1 - core)
            out.append(send(g_all.at[mine], g_all.at[mine], g_ss.at[13 + d], g_rs.at[13 + d], to))
        started.extend(out)
        return out

    def g_finish(cps):
        arrive(cps)
        for k in range(8):
            gwout_out[:, k * LANES : (k + 1) * LANES] = g_all[k]

    order = [("y", "z"), ("z", "y")]

    def slot(first_axis, second_axis, first_index, second_index):
        return first_index * 4 + second_index if first_axis == "y" else second_index * 4 + first_index

    def to_core(j):
        def body(k, _):
            core_send[j, k] = acc[j, k * 2 + 1 - core].astype(BF16)
            return 0

        lax.fori_loop(0, 16, body, 0)
        cp = send(core_send.at[j], core_recv.at[j], p_ss.at[j, 0], p_rs.at[j, 0], sibling)
        started.append(cp)
        return [cp]

    def to_first(j, cps):
        arrive(cps)
        a, b = order[j]
        for p in range(4):
            def body(q, _):
                k = slot(a, b, p, q)
                one_send[j, p, q] = (acc[j, k * 2 + core] + core_recv[j, k].astype(F32)).astype(BF16)
                return 0

            lax.fori_loop(0, 4, body, 0)
        return spread(
            a, lambda k: one_send.at[j, k], lambda d, own: one_recv.at[j, d - 1],
            p_ss.at[j, pl.ds(1, 3)], p_rs.at[j, pl.ds(1, 3)],
        )

    def to_second(j, cps):
        arrive(cps)
        a, b = order[j]

        def body(q, _):
            total = one_send[j, place[a], q].astype(F32)
            for d in range(3):
                total = total + one_recv[j, d, q].astype(F32)
            two_send[j, q] = total.astype(BF16)
            return 0

        lax.fori_loop(0, 4, body, 0)
        return spread(
            b, lambda k: two_send.at[j, k], lambda d, own: two_recv.at[j, d - 1],
            p_ss.at[j, pl.ds(4, 3)], p_rs.at[j, pl.ds(4, 3)],
        )

    def to_x(j, cps):
        arrive(cps)
        total = two_send[j, place[order[j][1]]].astype(F32)
        for d in range(3):
            total = total + two_recv[j, d].astype(F32)
        three[j, e] = total.astype(BF16)
        return spread(
            "x", lambda k: three.at[j, e], lambda d, own: three.at[j, own],
            p_ss.at[j, pl.ds(7, 3)], p_rs.at[j, pl.ds(7, 3)],
        )

    def finish(j, cps):
        arrive(cps)
        gwin_out[:, j * WIDE : (j + 1) * WIDE] = four(three.at[j]) / live_total

    outs = []

    def latent_tile(t):
        m, s = t // 2, pl.ds((t % 2) * CHUNK, CHUNK)
        lat[m, s, :] = dot(back[m, s, :], w[...], 1, 1).astype(BF16)
        cp = pltpu.make_async_copy(lat.at[m, s], glat_hbm.at[m, s], out_sem.at[t])
        cp.start()
        outs.append(cp)

    g = g_start()
    acc[0] += weight_piece(1, 0)
    p0 = to_core(0)
    g = g_to_y(g)
    arrive([lc])
    ls_y[y] = ls_core[0] + ls_core[1]
    lc = spread("y", lambda k: ls_y.at[y], lambda d, own: ls_y.at[own], t_ss.at[pl.ds(8, 3)], t_rs.at[pl.ds(8, 3)])
    acc[1] += weight_piece(1, 1)
    p1 = to_core(1)
    p0 = to_first(0, p0)
    latent_tile(0)
    p1 = to_first(1, p1)
    g = g_to_z(g)
    arrive(lc)
    ls_z[z] = four(ls_y)
    lc = spread("z", lambda k: ls_z.at[z], lambda d, own: ls_z.at[own], t_ss.at[pl.ds(11, 3)], t_rs.at[pl.ds(11, 3)])
    latent_tile(1)
    latent_tile(2)
    g = g_to_x(g)
    arrive(lc)
    ls_x[e] = four(ls_z)
    lc = spread("x", lambda k: ls_x.at[e], lambda d, own: ls_x.at[own], t_ss.at[pl.ds(14, 3)], t_rs.at[pl.ds(14, 3)])
    latent_tile(3)
    p0 = to_second(0, p0)
    p1 = to_second(1, p1)
    g = g_to_all(g)
    arrive(lc)
    loss_out[...] = jnp.sum(four(ls_x), axis=1, keepdims=True) / weight_total + jnp.zeros((8, LANES), F32)
    p0 = to_x(0, p0)
    p1 = to_x(1, p1)
    g_finish(g)
    finish(0, p0)
    finish(1, p1)
    for cp in started:
        cp.wait_send()
    for cp in outs:
        cp.wait()


def per_device(latent, w_in, output_weight, targets, area_weights, live_counts):
    vmem = pl.BlockSpec(memory_space=pltpu.VMEM)
    hbm = pl.BlockSpec(memory_space=pl.ANY)
    V = pltpu.VMEM
    dma = pltpu.SemaphoreType.DMA
    scratch = [
        V((2, POINTS, FEATURES), BF16),
        V((FEATURES, FEATURES), BF16),
        V((2, POINTS, FEATURES), BF16),
        V((2, POINTS, FEATURES), BF16),
        V((PIECES, 32, ROWS, WIDE), F32),
        V((CHUNKS, 4, 2, VARS, LANES), BF16),
        V((CHUNKS, 4, 2, VARS, LANES), BF16),
        V((CHUNKS, 4, 2, VARS, LANES), BF16),
        V((CHUNKS, 4, 2, VARS, LANES), BF16),
        V((VARS, FEATURES), F32),
        V((8, LANES), F32),
        V((PIECES, 16, ROWS, WIDE), BF16),
        V((PIECES, 16, ROWS, WIDE), BF16),
        V((PIECES, 4, 4, ROWS, WIDE), BF16),
        V((PIECES, 3, 4, ROWS, WIDE), BF16),
        V((PIECES, 4, ROWS, WIDE), BF16),
        V((PIECES, 3, ROWS, WIDE), BF16),
        V((PIECES, 4, ROWS, WIDE), BF16),
        V((4, VARS, LANES), BF16),
        V((4, VARS, LANES), BF16),
        V((4, VARS, LANES), BF16),
        V((3, VARS, LANES), BF16),
        V((4, VARS, LANES), BF16),
        V((4, VARS, LANES), BF16),
        V((8, VARS, LANES), F32),
        V((2, 8, LANES), F32),
        V((4, 8, LANES), F32),
        V((4, 8, LANES), F32),
        V((2, 8, LANES), F32),
        V((4, 8, LANES), F32),
        V((4, 8, LANES), F32),
        V((4, 8, LANES), F32),
        dma((5,)), dma((4,)),
        dma((CHUNKS, 2, 3)), dma((CHUNKS, 2, 3)),
        dma((CHUNKS, 3)), dma((CHUNKS, 3)),
        dma((PIECES, 10)), dma((PIECES, 10)),
        dma((17,)), dma((17,)),
        dma((17,)), dma((17,)),
    ]
    loss, glat, gwin, gwout = pl.pallas_call(
        kernel,
        out_shape=[
            jax.ShapeDtypeStruct((8, LANES), F32),
            jax.ShapeDtypeStruct(latent.shape, BF16),
            jax.ShapeDtypeStruct((ROWS, FEATURES), F32),
            jax.ShapeDtypeStruct((VARS, FEATURES), F32),
        ],
        in_specs=[hbm, hbm, vmem, vmem, vmem, pl.BlockSpec(memory_space=pltpu.SMEM)],
        out_specs=[vmem, hbm, vmem, vmem],
        scratch_shapes=scratch,
        compiler_params=pltpu.CompilerParams(collective_id=1, has_side_effects=True, vmem_limit_bytes=56 << 20),
        name="energy_step",
    )(latent, w_in, output_weight, targets, area_weights.reshape(8, LANES), live_counts)
    return loss[0, 0], glat, gwin, gwout


def solution(mesh):
    placed = (P("ens", "sp", None), P(), P(), P(None, "sp"), P("sp"), P("sp"))
    return jax.shard_map(
        per_device,
        mesh=mesh,
        in_specs=placed,
        out_specs=(P(), P("ens", "sp", None), P("sp", None), P()),
        check_vma=False,
    )
```

```python
import functools
import math

import jax
import jax.numpy as jnp
from jax import lax
from jax.experimental import pallas as pl
from jax.experimental.pallas import tpu as pltpu
from jax.sharding import PartitionSpec as P

BF16, F32 = jnp.bfloat16, jnp.float32
MESH = pl.DeviceIdType.MESH
LOSS_SCALE = 1024.0
MEMBERS, VARS, FEATURES, POINTS = 8, 80, 1024, 1024
CHUNKS = 2
CHUNK = POINTS // CHUNKS
LANES = 128
PIECES = 4
WIDE = FEATURES // PIECES
ROWS = 32
OUTER = math.sqrt(2.0 / math.pi)
INNER = OUTER * 0.044715


def dot(a, b, ca, cb):
    return lax.dot_general(a, b, (((ca,), (cb,)), ((), ())), preferred_element_type=F32)


def activation(z):
    cubic = INNER * (z * z)
    s = 0.5 * jnp.tanh(z * (cubic + OUTER)) + 0.5
    h = z * s
    slope = s + (h - h * s) * (6.0 * cubic + 2.0 * OUTER)
    return h.astype(BF16), slope.astype(BF16)


def activation_only(z):
    return (z * (0.5 * jnp.tanh(z * (INNER * (z * z) + OUTER)) + 0.5)).astype(BF16)


def score_block(x_ref, y, weighted, scales, store):
    n = MEMBERS
    pairs = [(i, j) for i in range(n) for j in range(i + 1, n)]
    step = 16
    own = [jnp.zeros((step, LANES), F32) for _ in range(n)]
    between = [jnp.zeros((step, LANES), F32) for _ in pairs]
    for v in range(0, VARS, step):
        x = [x_ref[m // 2, m % 2, v : v + step, :].astype(F32) for m in range(n)]
        for m in range(n):
            d = x[m] - y[v : v + step]
            own[m] = own[m] + d * d
        for q, (i, j) in enumerate(pairs):
            d = x[i] - x[j]
            between[q] = between[q] + d * d
    a = [jnp.sqrt(jnp.sum(o, axis=0, keepdims=True) + 1.0) for o in own]
    b = [jnp.sqrt(jnp.sum(o, axis=0, keepdims=True) + 1.0) for o in between]
    score = sum(a) / n - sum(b) / (n * (n - 1.0))
    from_target = [scales / (n * t) for t in a]
    from_pair = [scales / (n * (n - 1.0) * t) for t in b]
    for v in range(0, VARS, step):
        x = [x_ref[m // 2, m % 2, v : v + step, :].astype(F32) for m in range(n)]
        total = [(x[m] - y[v : v + step]) * from_target[m] for m in range(n)]
        for q, (i, j) in enumerate(pairs):
            d = (x[i] - x[j]) * from_pair[q]
            total[i] = total[i] - d
            total[j] = total[j] + d
        for m in range(n):
            store(m, v, step, total[m].astype(BF16))
    return weighted * score


def kernel(
    lat_hbm, w_hbm, wout_hbm, targets_hbm, area_hbm, live,
    loss_out, glat_out, gwin_out, gwout_out,
    lat, later, w, wout, targets, area, hid, back, acc, fsend, frecv, ssend, srecv, gout,
    core_send, core_recv, one_send, one_recv, two_send, two_recv, three,
    g_core_send, g_core_recv, g_y_send, g_y_recv, g_z, g_x, g_all,
    wt_near, wt_y, ls_core, ls_y, ls_z, ls_x,
    in_sem, f_ss, f_rs, s_ss, s_rs, p_ss, p_rs, g_ss, g_rs, t_ss, t_rs,
):
    e = lax.axis_index("ens")
    sp = lax.axis_index("sp")
    core = lax.rem(sp, 2)
    z = lax.rem(sp // 2, 4)
    y = sp // 8

    def turn(i, d):
        return lax.rem(i + d, 4)

    def device(x_, y_, z_, core_):
        return (x_, (y_ * 4 + z_) * 2 + core_)

    along = {
        "x": lambda d: device(turn(e, d), y, z, core),
        "y": lambda d: device(e, turn(y, d), z, core),
        "z": lambda d: device(e, y, turn(z, d), core),
    }
    place = {"x": e, "y": y, "z": z}
    sibling = device(e, y, z, 1 - core)

    def load(m, c):
        s = pl.ds(c * CHUNK, CHUNK)
        return pltpu.make_async_copy(lat_hbm.at[m, s], lat.at[m, s], in_sem.at[1 + 2 * c + m])

    load_w = [
        pltpu.make_async_copy(w_hbm.at[pl.ds(i * 256, 256)], w.at[pl.ds(i * 256, 256)], in_sem.at[8 + i])
        for i in range(4)
    ]
    for cp in load_w:
        cp.start()
    load(0, 0).start()
    small = [
        pltpu.make_async_copy(a, b, in_sem.at[5 + i])
        for i, (a, b) in enumerate([(area_hbm, area), (wout_hbm, wout), (targets_hbm, targets)])
    ]
    for cp in small:
        cp.start()
    loads = {(c, m): load(m, c) for c in range(CHUNKS) for m in range(2)}

    peers = [along[k](d) for k in "xyz" for d in (1, 2, 3)] + [sibling]
    peers += [device(turn(e, d), y, z, 1 - core) for d in (1, 2, 3)]
    across_z = [device(e, y, turn(z, d), 1 - core) for d in (1, 2, 3)]
    peers += across_z
    barrier = pltpu.get_barrier_semaphore()
    for p in peers:
        pl.semaphore_signal(barrier, inc=1, device_id=p, device_id_type=MESH)

    def send(src, dst, ss, rs, to):
        cp = pltpu.make_async_remote_copy(
            src_ref=src, dst_ref=dst, send_sem=ss, recv_sem=rs, device_id=to, device_id_type=MESH
        )
        cp.start()
        return cp

    started = []

    def spread(axis, src, dst, ss, rs, hops=(2, 1, 3)):
        cps = []
        for d in hops:
            cps.append(send(src(turn(place[axis], d)), dst(d, place[axis]), ss.at[d - 1], rs.at[d - 1], along[axis](d)))
        started.extend(cps)
        return cps

    def four(ref):
        return (ref[0].astype(F32) + ref[1].astype(F32)) + (ref[2].astype(F32) + ref[3].astype(F32))

    def arrive(cps):
        for cp in cps:
            cp.wait_recv()

    for cp in small:
        cp.wait()
    where = lax.broadcasted_iota(jnp.int32, (8, LANES), 0) * LANES + lax.broadcasted_iota(jnp.int32, (8, LANES), 1)
    is_live = (where < live[0]).astype(F32)
    weighted_all = area[...] * is_live
    first = lax.broadcasted_iota(jnp.int32, (8, LANES), 0) == 0
    wt_own = jnp.where(
        first, jnp.sum(weighted_all, axis=0, keepdims=True), jnp.sum(is_live, axis=0, keepdims=True)
    )
    wt_near[z * 2 + core] = wt_own

    def forward(c, m):
        s = pl.ds(c * CHUNK, CHUNK)
        pre = jnp.dot(lat[m, s, :], w[...], preferred_element_type=F32)
        if c == 0:
            hid[m, s, :], back[m, s, :] = activation(pre)
        else:
            hid[m, s, :] = activation_only(pre)
            later[m] = pre
        f = dot(wout[...], hid[m, s, :], 1, 1).astype(BF16)
        for k in range(4):
            fsend[c, k, m] = f[:, k * LANES : (k + 1) * LANES]
        frecv[c, e, m] = fsend[c, e, m]

    def forward_send(c, m, hops=(2, 1, 3)):
        return spread(
            "x", lambda k: fsend.at[c, k, m], lambda d, own: frecv.at[c, own, m], f_ss.at[c, m], f_rs.at[c, m], hops
        )

    def forward_half(c, m, hops):
        rows = [pl.ds(pl.multiple_of(c * CHUNK + turn(e, d) * LANES, LANES), LANES) for d in hops]
        pre = jnp.dot(
            jnp.concatenate([lat[m, r, :] for r in rows], axis=0), w[...], preferred_element_type=F32
        )
        h = activation_only(pre)
        for i, (r, d) in enumerate(zip(rows, hops)):
            hid[m, r, :] = h[i * LANES : (i + 1) * LANES]
            to = pl.ds(pl.multiple_of(turn(e, d) * LANES, LANES), LANES)
            later[m, to, :] = pre[i * LANES : (i + 1) * LANES]
        f = dot(wout[...], h, 1, 1).astype(BF16)
        for i, d in enumerate(hops):
            fsend[c, turn(e, d), m] = f[:, i * LANES : (i + 1) * LANES]

    loss_rows = []

    def scored(c):
        block = c * 4 + e
        y_block = targets[:, pl.ds(pl.multiple_of(block * LANES, LANES), LANES)].astype(F32)
        lanes = lax.broadcasted_iota(jnp.int32, (1, LANES), 1)
        weighted = area[pl.ds(block, 1), :] * (block * LANES + lanes < live[0]).astype(F32)
        scales = LOSS_SCALE * live_total * weighted / weight_total

        def store(m, v, step, value):
            ssend[c, m // 2, m % 2, v : v + step, :] = value

        loss_rows.append(score_block(frecv.at[c], y_block, weighted, scales, store))
        srecv[c, e] = ssend[c, e]
        return spread("x", lambda k: ssend.at[c, k], lambda d, own: srecv.at[c, own], s_ss.at[c], s_rs.at[c])

    def backward(c):
        s = pl.ds(c * CHUNK, CHUNK)
        for m in range(2):
            slopes = jnp.concatenate([srecv[c, k, m] for k in range(4)], axis=1)
            bh = dot(slopes, wout[...], 0, 0)
            back[m, s, :] = (back[m, s, :].astype(F32) * bh).astype(BF16)

    def output_part(c):
        s = pl.ds(c * CHUNK, CHUNK)
        slopes = jnp.concatenate([srecv[c, k, m] for m in range(2) for k in range(4)], axis=1)
        return dot(slopes, hid[:, s, :].reshape(2 * CHUNK, FEATURES), 1, 0)

    def weight_pieces(c, i):
        s, lo = pl.ds(c * CHUNK, CHUNK), 2 * i * WIDE
        a = lat[:, s, :].reshape(2 * CHUNK, FEATURES)
        both = dot(a, back[:, s, lo : lo + 2 * WIDE].reshape(2 * CHUNK, 2 * WIDE), 0, 0)
        for k in range(2):
            term = both[:, k * WIDE : (k + 1) * WIDE].reshape(16, 2, ROWS, WIDE)
            if c == 0:
                acc[2 * i + k] = term
            else:
                acc[2 * i + k] += term

    def g_start():
        def body(k, _):
            cols = pl.ds(pl.multiple_of((k * 2 + 1 - core) * LANES, LANES), LANES)
            g_core_send[k] = gout[:, cols].astype(BF16)
            return 0

        lax.fori_loop(0, 4, body, 0)
        cp = send(g_core_send, g_core_recv, g_ss.at[0], g_rs.at[0], sibling)
        started.append(cp)
        return [cp]

    def g_to_first(cps):
        arrive(cps)

        def body(k, _):
            cols = pl.ds(pl.multiple_of((k * 2 + core) * LANES, LANES), LANES)
            g_y_send[k] = (gout[:, cols] + g_core_recv[k].astype(F32)).astype(BF16)
            return 0

        lax.fori_loop(0, 4, body, 0)
        return spread(
            "x", lambda k: g_y_send.at[k], lambda d, own: g_y_recv.at[d - 1], g_ss.at[pl.ds(1, 3)], g_rs.at[pl.ds(1, 3)]
        )

    def g_to_second(cps):
        arrive(cps)
        total = g_y_send[e].astype(F32)
        for d in range(3):
            total = total + g_y_recv[d].astype(F32)
        g_z[y] = total.astype(BF16)
        return spread(
            "y", lambda k: g_z.at[y], lambda d, own: g_z.at[own], g_ss.at[pl.ds(4, 3)], g_rs.at[pl.ds(4, 3)]
        )

    def g_to_third(cps):
        arrive(cps)
        g_x[z] = four(g_z).astype(BF16)
        return spread(
            "z", lambda k: g_x.at[z], lambda d, own: g_x.at[own], g_ss.at[pl.ds(7, 3)], g_rs.at[pl.ds(7, 3)]
        )

    def g_to_all(cps):
        arrive(cps)
        mine = e * 2 + core
        g_all[mine] = (four(g_x) / live_total).astype(BF16)
        out = [send(g_all.at[mine], g_all.at[mine], g_ss.at[10], g_rs.at[10], sibling)]
        for d in (1, 2, 3):
            out.append(send(g_all.at[mine], g_all.at[mine], g_ss.at[10 + d], g_rs.at[10 + d], along["x"](d)))
        for d in (1, 2, 3):
            to = device(turn(e, d), y, z, 1 - core)
            out.append(send(g_all.at[mine], g_all.at[mine], g_ss.at[13 + d], g_rs.at[13 + d], to))
        started.extend(out)
        return out

    def g_finish(cps):
        arrive(cps)
        for k in range(8):
            gwout_out[:, k * LANES : (k + 1) * LANES] = g_all[k].astype(F32)

    order = [("y", "z"), ("z", "y")] * (PIECES // 2)

    def to_core(j):
        core_send[j] = acc[j, :, 1 - core].astype(BF16)
        cp = send(core_send.at[j], core_recv.at[j], p_ss.at[j, 0], p_rs.at[j, 0], sibling)
        started.append(cp)
        return [cp]

    def part(j, k):
        return one_send.at[j, k] if order[j][0] == "y" else one_send.at[j, :, k]

    def to_first(j, cps):
        arrive(cps)
        one_send[j] = (acc[j, :, core] + core_recv[j].astype(F32)).astype(BF16).reshape(4, 4, ROWS, WIDE)
        return spread(
            order[j][0], lambda k: part(j, k), lambda d, own: one_recv.at[j, d - 1],
            p_ss.at[j, pl.ds(1, 3)], p_rs.at[j, pl.ds(1, 3)],
        )

    def to_second(j, cps):
        arrive(cps)
        total = part(j, place[order[j][0]])[...].astype(F32)
        for d in range(3):
            total = total + one_recv[j, d].astype(F32)
        two_send[j] = total.astype(BF16)
        return spread(
            order[j][1], lambda k: two_send.at[j, k], lambda d, own: two_recv.at[j, d - 1],
            p_ss.at[j, pl.ds(4, 3)], p_rs.at[j, pl.ds(4, 3)],
        )

    def to_x(j, cps):
        arrive(cps)
        total = two_send[j, place[order[j][1]]].astype(F32)
        for d in range(3):
            total = total + two_recv[j, d].astype(F32)
        three[j, e] = total.astype(BF16)
        return spread(
            "x", lambda k: three.at[j, e], lambda d, own: three.at[j, own],
            p_ss.at[j, pl.ds(7, 3)], p_rs.at[j, pl.ds(7, 3)],
        )

    def finish(j, cps):
        arrive(cps)
        gwin_out[:, j * WIDE : (j + 1) * WIDE] = four(three.at[j]) / live_total

    def latent_tile(t):
        m, s = t // 2, pl.ds((t % 2) * CHUNK, CHUNK)
        glat_out[m, s, :] = dot(back[m, s, :], w[...], 1, 1).astype(BF16)

    for cp in load_w:
        cp.wait()
    loads[0, 0].wait()
    for key in ((0, 1), (1, 0), (1, 1)):
        loads[key].start()
    forward(0, 0)
    pl.semaphore_wait(barrier, len(peers))
    f00 = forward_send(0, 0)
    mine = z * 2 + core
    tw = []
    for i, to in enumerate([sibling] + [along["z"](d) for d in (1, 2, 3)] + across_z):
        tw.append(send(wt_near.at[mine], wt_near.at[mine], t_ss.at[17 + i], t_rs.at[17 + i], to))
    started.extend(tw)
    loads[0, 1].wait()
    forward(0, 1)
    f01 = forward_send(0, 1)
    arrive(tw)
    near = wt_near[0]
    for i in range(1, 8):
        near = near + wt_near[i]
    wt_y[y] = near
    tw = spread("y", lambda k: wt_y.at[y], lambda d, own: wt_y.at[own], t_ss.at[pl.ds(4, 3)], t_rs.at[pl.ds(4, 3)])
    loads[1, 0].wait()
    forward(1, 0)
    f10 = forward_send(1, 0)
    loads[1, 1].wait()
    forward_half(1, 1, (2, 1))
    f11 = forward_send(1, 1, (2, 1))
    arrive(tw)
    totals = jnp.sum(four(wt_y), axis=1, keepdims=True)
    weight_total = totals[0:1, 0:1]
    live_total = totals[1:2, 0:1]
    arrive(f00)
    arrive(f01)
    s0 = scored(0)
    forward_half(1, 1, (3, 0))
    f11 += forward_send(1, 1, (3,))
    frecv[1, e, 1] = fsend[1, e, 1]
    for m in range(2):
        back[m, CHUNK:, :] = activation(later[m])[1]
    arrive(f10)
    arrive(f11)
    s1 = scored(1)
    ls_core[core] = jnp.broadcast_to(loss_rows[0] + loss_rows[1], (8, LANES))
    lc = send(ls_core.at[core], ls_core.at[core], t_ss.at[7], t_rs.at[7], sibling)
    started.append(lc)
    arrive(s0)
    backward(0)
    gout[...] = output_part(0)
    arrive([lc])
    ls_y[y] = ls_core[0] + ls_core[1]
    lc = spread("y", lambda k: ls_y.at[y], lambda d, own: ls_y.at[own], t_ss.at[pl.ds(8, 3)], t_rs.at[pl.ds(8, 3)])
    weight_pieces(0, 0)
    weight_pieces(0, 1)
    arrive(s1)
    gout[...] += output_part(1)
    g = g_start()
    backward(1)
    g = g_to_first(g)
    weight_pieces(1, 0)
    p0 = to_core(0)
    p1 = to_core(1)
    arrive(lc)
    ls_z[z] = four(ls_y)
    lc = spread("z", lambda k: ls_z.at[z], lambda d, own: ls_z.at[own], t_ss.at[pl.ds(11, 3)], t_rs.at[pl.ds(11, 3)])
    weight_pieces(1, 1)
    p2 = to_core(2)
    p3 = to_core(3)
    g = g_to_second(g)
    p0 = to_first(0, p0)
    p1 = to_first(1, p1)
    latent_tile(0)
    p2 = to_first(2, p2)
    p3 = to_first(3, p3)
    latent_tile(1)
    g = g_to_third(g)
    arrive(lc)
    ls_x[e] = four(ls_z)
    lc = spread("x", lambda k: ls_x.at[e], lambda d, own: ls_x.at[own], t_ss.at[pl.ds(14, 3)], t_rs.at[pl.ds(14, 3)])
    latent_tile(2)
    p0 = to_second(0, p0)
    p1 = to_second(1, p1)
    latent_tile(3)
    p2 = to_second(2, p2)
    p3 = to_second(3, p3)
    g = g_to_all(g)
    arrive(lc)
    loss_out[...] = jnp.sum(four(ls_x), axis=1, keepdims=True) / weight_total + jnp.zeros((8, LANES), F32)
    p0 = to_x(0, p0)
    p1 = to_x(1, p1)
    p2 = to_x(2, p2)
    p3 = to_x(3, p3)
    g_finish(g)
    finish(0, p0)
    finish(1, p1)
    finish(2, p2)
    finish(3, p3)
    for cp in started:
        cp.wait_send()


def write_out(loss, glat, gwin, gwout, loss_out, glat_out, gwin_out, gwout_out, sem):
    cps = [pltpu.make_async_copy(gwin, gwin_out, sem.at[0]), pltpu.make_async_copy(gwout, gwout_out, sem.at[1])]
    for i in range(16):
        m, s = i // 8, pl.ds((i % 8) * LANES, LANES)
        cps.append(pltpu.make_async_copy(glat.at[m, s], glat_out.at[m, s], sem.at[2 + i]))
    for cp in cps:
        cp.start()
    loss_out[...] = loss[0:1, 0:1]
    for cp in cps:
        cp.wait()


def per_device(latent, w_in, output_weight, targets, area_weights, live_counts):
    vmem = pl.BlockSpec(memory_space=pltpu.VMEM)
    hbm = pl.BlockSpec(memory_space=pl.ANY)
    V = pltpu.VMEM
    dma = pltpu.SemaphoreType.DMA
    scratch = [
        V((2, POINTS, FEATURES), BF16),
        V((2, CHUNK, FEATURES), F32),
        V((FEATURES, FEATURES), BF16),
        V((VARS, FEATURES), BF16),
        V((VARS, POINTS), BF16),
        V((8, LANES), F32),
        V((2, POINTS, FEATURES), BF16),
        V((2, POINTS, FEATURES), BF16),
        V((PIECES, 16, 2, ROWS, WIDE), F32),
        V((CHUNKS, 4, 2, VARS, LANES), BF16),
        V((CHUNKS, 4, 2, VARS, LANES), BF16),
        V((CHUNKS, 4, 2, VARS, LANES), BF16),
        V((CHUNKS, 4, 2, VARS, LANES), BF16),
        V((VARS, FEATURES), F32),
        V((PIECES, 16, ROWS, WIDE), BF16),
        V((PIECES, 16, ROWS, WIDE), BF16),
        V((PIECES, 4, 4, ROWS, WIDE), BF16),
        V((PIECES, 3, 4, ROWS, WIDE), BF16),
        V((PIECES, 4, ROWS, WIDE), BF16),
        V((PIECES, 3, ROWS, WIDE), BF16),
        V((PIECES, 4, ROWS, WIDE), BF16),
        V((4, VARS, LANES), BF16),
        V((4, VARS, LANES), BF16),
        V((4, VARS, LANES), BF16),
        V((3, VARS, LANES), BF16),
        V((4, VARS, LANES), BF16),
        V((4, VARS, LANES), BF16),
        V((8, VARS, LANES), BF16),
        V((8, 8, LANES), F32),
        V((4, 8, LANES), F32),
        V((2, 8, LANES), F32),
        V((4, 8, LANES), F32),
        V((4, 8, LANES), F32),
        V((4, 8, LANES), F32),
        dma((12,)),
        dma((CHUNKS, 2, 3)), dma((CHUNKS, 2, 3)),
        dma((CHUNKS, 3)), dma((CHUNKS, 3)),
        dma((PIECES, 10)), dma((PIECES, 10)),
        dma((17,)), dma((17,)),
        dma((24,)), dma((24,)),
    ]
    operands = (latent, w_in, output_weight, targets, area_weights.reshape(8, LANES))
    results = pl.pallas_call(
        kernel,
        out_shape=[
            V((8, LANES), F32),
            V(latent.shape, BF16),
            V((ROWS, FEATURES), F32),
            V((VARS, FEATURES), F32),
        ],
        in_specs=[pl.BlockSpec(memory_space=pltpu.HBM)] * 5 + [pl.BlockSpec(memory_space=pltpu.SMEM)],
        out_specs=[vmem] * 4,
        scratch_shapes=scratch,
        compiler_params=pltpu.CompilerParams(collective_id=1, has_side_effects=True, vmem_limit_bytes=48 << 20),
        name="energy_step",
    )(*[pltpu.with_memory_space_constraint(a, pltpu.HBM) for a in operands], live_counts)
    loss, glat, gwin, gwout = pl.pallas_call(
        write_out,
        out_shape=[
            jax.ShapeDtypeStruct((1, 1), F32),
            jax.ShapeDtypeStruct(latent.shape, BF16),
            jax.ShapeDtypeStruct((ROWS, FEATURES), F32),
            jax.ShapeDtypeStruct((VARS, FEATURES), F32),
        ],
        in_specs=[vmem] * 4,
        out_specs=[vmem] + [hbm] * 3,
        scratch_shapes=[dma((18,))],
        compiler_params=pltpu.CompilerParams(vmem_limit_bytes=1 << 20),
        name="write_out",
    )(*[pltpu.with_memory_space_constraint(r, pltpu.VMEM) for r in results])
    return loss.reshape(()), glat, gwin, gwout


def solution(mesh):
    placed = (P("ens", "sp", None), P(), P(), P(None, "sp"), P("sp"), P("sp"))
    return jax.shard_map(
        per_device,
        mesh=mesh,
        in_specs=placed,
        out_specs=(P(), P("ens", "sp", None), P("sp", None), P()),
        check_vma=False,
    )
```

```python
import functools
import math

import jax
import jax.numpy as jnp
from jax import lax
from jax.experimental import pallas as pl
from jax.experimental.pallas import tpu as pltpu
from jax.sharding import PartitionSpec as P

BF16, F32 = jnp.bfloat16, jnp.float32
MESH = pl.DeviceIdType.MESH
LOSS_SCALE = 1024.0
MEMBERS, VARS, FEATURES, POINTS = 8, 80, 1024, 1024
CHUNKS = 2
CHUNK = POINTS // CHUNKS
LANES = 128
HALF = FEATURES // 2
PIECES = ((0, 256, 128, "y"), (0, 384, 128, "z"), (1, 0, 256, "y"), (1, 256, 256, "z"))
SENDS = 8
FAR = ((2, 2), (2, 1), (2, 3), (1, 2), (3, 2))
ROWS = 32
OUTER = math.sqrt(2.0 / math.pi)
INNER = OUTER * 0.044715


def dot(a, b, ca, cb):
    return lax.dot_general(a, b, (((ca,), (cb,)), ((), ())), preferred_element_type=F32)


def activation(z):
    cubic = INNER * (z * z)
    s = 0.5 * jnp.tanh(z * (cubic + OUTER)) + 0.5
    h = z * s
    slope = s + (h - h * s) * (6.0 * cubic + 2.0 * OUTER)
    return h.astype(BF16), slope.astype(BF16)


def activation_only(z):
    return (z * (0.5 * jnp.tanh(z * (INNER * (z * z) + OUTER)) + 0.5)).astype(BF16)


def score_block(x_ref, y, weighted, scales, store):
    n = MEMBERS
    pairs = [(i, j) for i in range(n) for j in range(i + 1, n)]
    step = 16
    own = [jnp.zeros((step, LANES), F32) for _ in range(n)]
    between = [jnp.zeros((step, LANES), F32) for _ in pairs]
    for v in range(0, VARS, step):
        x = [x_ref[m // 2, m % 2, v : v + step, :].astype(F32) for m in range(n)]
        for m in range(n):
            d = x[m] - y[v : v + step]
            own[m] = own[m] + d * d
        for q, (i, j) in enumerate(pairs):
            d = x[i] - x[j]
            between[q] = between[q] + d * d
    a = [jnp.sqrt(jnp.sum(o, axis=0, keepdims=True) + 1.0) for o in own]
    b = [jnp.sqrt(jnp.sum(o, axis=0, keepdims=True) + 1.0) for o in between]
    score = sum(a) / n - sum(b) / (n * (n - 1.0))
    from_target = [scales / (n * t) for t in a]
    from_pair = [scales / (n * (n - 1.0) * t) for t in b]
    for v in range(0, VARS, step):
        x = [x_ref[m // 2, m % 2, v : v + step, :].astype(F32) for m in range(n)]
        total = [(x[m] - y[v : v + step]) * from_target[m] for m in range(n)]
        for q, (i, j) in enumerate(pairs):
            d = (x[i] - x[j]) * from_pair[q]
            total[i] = total[i] - d
            total[j] = total[j] + d
        for m in range(n):
            store(m, v, step, total[m].astype(BF16))
    return weighted * score


def kernel(
    lat_hbm, w_hbm, wout_hbm, targets_hbm, area_hbm, live,
    loss_out, glat_out, gwin_out, gwout_out,
    lat, later, w, wout, targets, area, hid, back, acc, fsend, frecv, ssend, srecv, gout,
    core_send, core_recv, one_send, one_recv, two_send, two_recv, three,
    x_send, x_recv, xy_send, xy_recv, xz_send, x_all,
    g_core_send, g_core_recv, g_one_send, g_one_recv, g_two, g_three, g_all,
    wt_near, wt_y, ls_core, ls_y, ls_z, ls_x,
    in_sem, out_sem, f_rs, s_rs, p_rs, g_rs, t_rs,
):
    e = lax.axis_index("ens")
    sp = lax.axis_index("sp")
    core = lax.rem(sp, 2)
    z = lax.rem(sp // 2, 4)
    y = sp // 8

    def turn(i, d):
        return lax.rem(i + d, 4)

    def device(x_, y_, z_, core_):
        return (x_, (y_ * 4 + z_) * 2 + core_)

    along = {
        "x": lambda d: device(turn(e, d), y, z, core),
        "y": lambda d: device(e, turn(y, d), z, core),
        "z": lambda d: device(e, y, turn(z, d), core),
    }
    place = {"x": e, "y": y, "z": z}
    sibling = device(e, y, z, 1 - core)
    across_x = [device(turn(e, d), y, z, 1 - core) for d in (1, 2, 3)]
    across_z = [device(e, y, turn(z, d), 1 - core) for d in (1, 2, 3)]

    def load(m, c):
        s = pl.ds(c * CHUNK, CHUNK)
        return pltpu.make_async_copy(lat_hbm.at[m, s], lat.at[m, s], in_sem.at[2 * c + m])

    loads = {(c, m): load(m, c) for c in range(CHUNKS) for m in range(2)}
    loads[0, 0].start()
    load_w = []
    for i in range(2):
        cols = pl.ds(i * HALF, HALF)
        load_w.append(pltpu.make_async_copy(w_hbm.at[:, cols], w.at[:, cols], in_sem.at[4 + i]))
        load_w[i].start()
    small = [
        pltpu.make_async_copy(src, dst, in_sem.at[8 + i])
        for i, (src, dst) in enumerate([(area_hbm, area), (wout_hbm, wout), (targets_hbm, targets)])
    ]
    for cp in small:
        cp.start()

    peers = [along[k](d) for k in "xyz" for d in (1, 2, 3)] + [sibling] + across_x + across_z
    peers += [device(turn(e, dx), y, turn(z, dz), core) for dx in (1, 2, 3) for dz in (1, 2, 3)]
    barrier = pltpu.get_barrier_semaphore()
    for p in peers:
        pl.semaphore_signal(barrier, inc=1, device_id=p, device_id_type=MESH)

    def remote(src, dst, ss, rs, to):
        return pltpu.make_async_remote_copy(
            src_ref=src, dst_ref=dst, send_sem=ss, recv_sem=rs, device_id=to, device_id_type=MESH
        )

    leaving = {}
    turns = [0]

    def send(copies, rs, whole, sent=None):
        k = turns[0] % SENDS
        turns[0] += 1
        if k in leaving:
            leaving.pop(k)()
        ss = out_sem.at[k]
        for src, dst, to in copies:
            remote(src, dst, ss, rs, to).start()
        sent = whole if sent is None else sent
        leaving[k] = lambda: remote(sent, sent, ss, rs, sibling).wait_send()
        return lambda: remote(whole, whole, ss, rs, sibling).wait_recv()

    def spread(axis, src, dst, rs, whole, sent=None, hops=(2, 1, 3)):
        own = place[axis]
        return send([(src(turn(own, d)), dst(d, own), along[axis](d)) for d in hops], rs, whole, sent)

    def share(axis, buf, rs):
        return spread(axis, lambda k: buf.at[place[axis]], lambda d, own: buf.at[own], rs, buf.at[pl.ds(0, 3)])

    def four(ref):
        return (ref[0].astype(F32) + ref[1].astype(F32)) + (ref[2].astype(F32) + ref[3].astype(F32))

    def received(own, ref):
        total = own.astype(F32)
        for d in range(3):
            total = total + ref[d].astype(F32)
        return total

    for cp in small:
        cp.wait()
    where = lax.broadcasted_iota(jnp.int32, (8, LANES), 0) * LANES + lax.broadcasted_iota(jnp.int32, (8, LANES), 1)
    is_live = (where < live[0]).astype(F32)
    weighted_all = area[...] * is_live
    first = lax.broadcasted_iota(jnp.int32, (8, LANES), 0) == 0
    near_slot = z * 2 + core
    wt_near[near_slot] = jnp.where(
        first, jnp.sum(weighted_all, axis=0, keepdims=True), jnp.sum(is_live, axis=0, keepdims=True)
    )

    def forecast(c, m):
        f = dot(wout[...], hid[m, c * CHUNK : (c + 1) * CHUNK, :], 1, 1).astype(BF16)
        for k in range(4):
            fsend[c, k, m] = f[:, k * LANES : (k + 1) * LANES]
        frecv[c, e, m] = fsend[c, e, m]

    def forward(c, m):
        s = pl.ds(c * CHUNK, CHUNK)
        pre = jnp.dot(lat[m, s, :], w[...], preferred_element_type=F32)
        if c == 0:
            hid[m, s, :], back[m, s, :] = activation(pre)
        else:
            hid[m, s, :] = activation_only(pre)
            later[m] = pre
        forecast(c, m)

    def forward_send(c, m, hops=(2, 1, 3)):
        return spread(
            "x", lambda k: fsend.at[c, k, m], lambda d, own: frecv.at[c, own, m], f_rs.at[c, m],
            frecv.at[c, pl.ds(0, 3), m], frecv.at[c, pl.ds(0, len(hops)), m], hops,
        )

    def forward_half(c, m, hops):
        rows = [pl.ds(pl.multiple_of(c * CHUNK + turn(e, d) * LANES, LANES), LANES) for d in hops]
        pre = jnp.dot(
            jnp.concatenate([lat[m, r, :] for r in rows], axis=0), w[...], preferred_element_type=F32
        )
        h = activation_only(pre)
        for i, (r, d) in enumerate(zip(rows, hops)):
            hid[m, r, :] = h[i * LANES : (i + 1) * LANES]
            to = pl.ds(pl.multiple_of(turn(e, d) * LANES, LANES), LANES)
            later[m, to, :] = pre[i * LANES : (i + 1) * LANES]
        f = dot(wout[...], h, 1, 1).astype(BF16)
        for i, d in enumerate(hops):
            fsend[c, turn(e, d), m] = f[:, i * LANES : (i + 1) * LANES]

    def scored(c, weight_total, live_total):
        block = c * 4 + e
        y_block = targets[:, pl.ds(pl.multiple_of(block * LANES, LANES), LANES)].astype(F32)
        lanes = lax.broadcasted_iota(jnp.int32, (1, LANES), 1)
        weighted = area[pl.ds(block, 1), :] * (block * LANES + lanes < live[0]).astype(F32)
        scales = LOSS_SCALE * live_total * weighted / weight_total

        def store(m, v, step, value):
            ssend[c, m // 2, m % 2, v : v + step, :] = value

        row = score_block(frecv.at[c], y_block, weighted, scales, store)
        srecv[c, e] = ssend[c, e]
        return row

    def scored_send(c):
        return spread(
            "x", lambda k: ssend.at[c, k], lambda d, own: srecv.at[c, own], s_rs.at[c], srecv.at[c, pl.ds(0, 3)]
        )

    def backward(c, lo, wide):
        s, cols = pl.ds(c * CHUNK, CHUNK), slice(lo, lo + wide)
        for m in range(2):
            slopes = jnp.concatenate([srecv[c, k, m] for k in range(4)], axis=1)
            bh = dot(slopes, wout[:, cols], 0, 0)
            back[m, s, cols] = (back[m, s, cols].astype(F32) * bh).astype(BF16)

    def output_part(c):
        s = pl.ds(c * CHUNK, CHUNK)
        slopes = jnp.concatenate([srecv[c, k, m] for m in range(2) for k in range(4)], axis=1)
        return dot(slopes, hid[:, s, :].reshape(2 * CHUNK, FEATURES), 1, 0)

    def weight_half(c, i):
        s, cols = pl.ds(c * CHUNK, CHUNK), slice(i * HALF, (i + 1) * HALF)
        a = lat[:, s, :].reshape(2 * CHUNK, FEATURES)
        term = dot(a, back[:, s, cols].reshape(2 * CHUNK, HALF), 0, 0).reshape(16, 2, ROWS, HALF)
        if c == 0:
            acc[i] = term
        else:
            acc[i] += term

    def g_start():
        def body(k, _):
            cols = pl.ds(pl.multiple_of((k * 2 + 1 - core) * LANES, LANES), LANES)
            g_core_send[k] = gout[:, cols].astype(BF16)
            return 0

        lax.fori_loop(0, 4, body, 0)
        return send([(g_core_send, g_core_recv, sibling)], g_rs.at[0], g_core_recv)

    def g_to_first(arrived):
        arrived()

        def body(k, _):
            cols = pl.ds(pl.multiple_of((k * 2 + core) * LANES, LANES), LANES)
            g_one_send[k] = (gout[:, cols] + g_core_recv[k].astype(F32)).astype(BF16)
            return 0

        lax.fori_loop(0, 4, body, 0)
        return spread("x", lambda k: g_one_send.at[k], lambda d, own: g_one_recv.at[d - 1], g_rs.at[1], g_one_recv)

    def g_to_second(arrived):
        arrived()
        g_two[y] = received(g_one_send[e], g_one_recv).astype(BF16)
        return share("y", g_two, g_rs.at[2])

    def g_to_third(arrived):
        arrived()
        g_three[z] = four(g_two).astype(BF16)
        return share("z", g_three, g_rs.at[3])

    def g_to_all(arrived, live_total):
        arrived()
        mine = e * 2 + core
        g_all[mine] = (four(g_three) / live_total).astype(BF16)
        to = [along["x"](d) for d in (2, 1, 3)] + across_x + [sibling]
        return send([(g_all.at[mine], g_all.at[mine], p) for p in to], g_rs.at[4], g_all.at[pl.ds(0, 7)])

    def g_finish(arrived):
        arrived()
        for k in range(8):
            gwout_out[:, k * LANES : (k + 1) * LANES] = g_all[k].astype(F32)

    def to_core(i):
        core_send[i] = acc[i, :, 1 - core].astype(BF16)
        return send([(core_send.at[i], core_recv.at[i], sibling)], p_rs.at[i], core_recv.at[i])

    def from_core(i, lo, wide):
        cols = slice(lo, lo + wide)
        return (acc[i, :, core, :, cols] + core_recv[i, :, :, cols].astype(F32)).astype(BF16)

    def part(j, k):
        return one_send[j].at[k] if PIECES[j][3] == "y" else one_send[j].at[:, k]

    def to_first(j):
        half, lo, wide, axis = PIECES[j]
        one_send[j][...] = from_core(half, lo, wide).reshape(4, 4, ROWS, wide)
        return spread(
            axis, lambda k: part(j, k), lambda d, own: one_recv[j].at[d - 1], p_rs.at[2 + j], one_recv[j]
        )

    def to_second(j, arrived):
        arrived()
        axis = PIECES[j][3]
        two_send[j][...] = received(part(j, place[axis])[...], one_recv[j]).astype(BF16)
        return spread(
            "z" if axis == "y" else "y", lambda k: two_send[j].at[k], lambda d, own: two_recv[j].at[d - 1],
            p_rs.at[6 + j], two_recv[j],
        )

    def to_third(i, arrived):
        for j in (2 * i, 2 * i + 1):
            arrived[j]()
            wide, own = PIECES[j][2], place["z" if PIECES[j][3] == "y" else "y"]
            lo = (j % 2) * wide
            three[i][e, :, lo : lo + wide] = received(two_send[j][own], two_recv[j]).astype(BF16)
        return share("x", three[i], p_rs.at[10 + i])

    def finish(i, arrived, live_total):
        arrived()
        wide = 2 * PIECES[2 * i][2]
        gwin_out[:, FEATURES // 4 * (1 + i) : FEATURES // 4 * (1 + i) + wide] = four(three[i]) / live_total

    def x_block(k):
        return slice((k // 2) * 16, (k // 2 + 1) * 16), slice((k % 2) * LANES, (k % 2 + 1) * LANES)

    def x_first():
        total = from_core(0, 0, 2 * LANES)
        for k in range(4):
            rows, cols = x_block(k)
            x_send[k] = total[:, rows, cols]
        return spread("x", lambda k: x_send.at[k], lambda d, own: x_recv.at[d - 1], p_rs.at[12], x_recv)

    def x_second(arrived):
        arrived()
        xy_send[...] = received(x_send[e], x_recv).astype(BF16).reshape(4, 4, 16, LANES)
        return spread("y", lambda k: xy_send.at[k], lambda d, own: xy_recv.at[d - 1], p_rs.at[13], xy_recv)

    def x_third(arrived):
        arrived()
        xz_send[...] = received(xy_send[y], xy_recv).astype(BF16)
        slot = e * 4 + z
        x_all[slot] = xz_send[z]
        copies = []
        for dx, dz in sorted(((i, j) for i in range(4) for j in range(4) if i or j), key=lambda h: h not in FAR):
            to = turn(z, dz)
            copies.append((xz_send.at[to], x_all.at[slot], device(turn(e, dx), y, to, core)))
        return send(copies, p_rs.at[14], x_all.at[pl.ds(0, 15)])

    def x_finish(arrived, live_total):
        arrived()
        for k in range(4):
            rows, cols = x_block(k)
            gwin_out[rows, cols] = four(x_all.at[pl.ds(4 * k, 4)]) / live_total

    def latent_tile(i):
        m, s = i // 2, pl.ds((i % 2) * CHUNK, CHUNK)
        glat_out[m, s, :] = dot(back[m, s, :], w[...], 1, 1).astype(BF16)

    loads[0, 0].wait()
    load_w[0].wait()
    loads[0, 1].start()
    for i in range(2):
        cols = slice(i * HALF, (i + 1) * HALF)
        if i == 1:
            load_w[1].wait()
            loads[1, 0].start()
            loads[1, 1].start()
        pre00 = jnp.dot(lat[0, :CHUNK, :], w[:, cols], preferred_element_type=F32)
        hid[0, :CHUNK, cols], back[0, :CHUNK, cols] = activation(pre00)
    forecast(0, 0)
    pl.semaphore_wait(barrier, len(peers))
    f00 = forward_send(0, 0)
    tw = send(
        [(wt_near.at[near_slot], wt_near.at[near_slot], p) for p in [along["z"](d) for d in (2, 1, 3)] + across_z + [sibling]],
        t_rs.at[0], wt_near.at[pl.ds(0, 7)],
    )
    loads[0, 1].wait()
    forward(0, 1)
    f01 = forward_send(0, 1)
    tw()
    near = wt_near[0]
    for i in range(1, 8):
        near = near + wt_near[i]
    wt_y[y] = near
    tw = share("y", wt_y, t_rs.at[1])
    loads[1, 0].wait()
    forward(1, 0)
    f10 = forward_send(1, 0)
    loads[1, 1].wait()
    forward_half(1, 1, (2, 1))
    f11 = forward_send(1, 1, (2, 1))
    tw()
    totals = jnp.sum(four(wt_y), axis=1, keepdims=True)
    weight_total, live_total = totals[0:1, 0:1], totals[1:2, 0:1]
    f00()
    f01()
    row0 = scored(0, weight_total, live_total)
    s0 = scored_send(0)
    forward_half(1, 1, (3, 0))
    forward_send(1, 1, (3,))
    frecv[1, e, 1] = fsend[1, e, 1]
    for m in range(2):
        back[m, CHUNK:, :] = activation(later[m])[1]
    f10()
    f11()
    row1 = scored(1, weight_total, live_total)
    s1 = scored_send(1)
    ls_core[core] = jnp.broadcast_to(row0 + row1, (8, LANES))
    lc = send([(ls_core.at[core], ls_core.at[core], sibling)], t_rs.at[2], ls_core.at[0])
    s0()
    backward(0, 0, FEATURES)
    gout[...] = output_part(0)
    weight_half(0, 0)
    lc()
    ls_y[y] = ls_core[0] + ls_core[1]
    lc = share("y", ls_y, t_rs.at[3])
    weight_half(0, 1)
    s1()
    gout[...] += output_part(1)
    g = g_start()
    backward(1, 0, HALF)
    weight_half(1, 0)
    c0 = to_core(0)
    g = g_to_first(g)
    lc()
    ls_z[z] = four(ls_y)
    lc = share("z", ls_z, t_rs.at[4])
    backward(1, HALF, HALF)
    weight_half(1, 1)
    c1 = to_core(1)
    c0()
    p = {}
    xf = x_first()
    p[0] = to_first(0)
    p[1] = to_first(1)
    latent_tile(0)
    g = g_to_second(g)
    c1()
    p[2] = to_first(2)
    p[3] = to_first(3)
    latent_tile(1)
    lc()
    ls_x[e] = four(ls_z)
    lc = share("x", ls_x, t_rs.at[5])
    latent_tile(2)
    latent_tile(3)
    xf = x_second(xf)
    p[0] = to_second(0, p[0])
    p[1] = to_second(1, p[1])
    g = g_to_third(g)
    lc()
    loss_out[...] = jnp.sum(four(ls_x), axis=1, keepdims=True) / weight_total + jnp.zeros((8, LANES), F32)
    p[2] = to_second(2, p[2])
    p[3] = to_second(3, p[3])
    xf = x_third(xf)
    xa = to_third(0, p)
    g = g_to_all(g, live_total)
    xb = to_third(1, p)
    finish(0, xa, live_total)
    x_finish(xf, live_total)
    g_finish(g)
    finish(1, xb, live_total)
    for left in leaving.values():
        left()


def write_out(loss, glat, gwin, gwout, loss_out, glat_out, gwin_out, gwout_out, sem):
    pairs = [(glat, glat_out), (gwin, gwin_out), (gwout, gwout_out)]
    cps = [pltpu.make_async_copy(src, dst, sem.at[i]) for i, (src, dst) in enumerate(pairs)]
    for cp in cps:
        cp.start()
    loss_out[...] = loss[0:1, 0:1]
    for cp in cps:
        cp.wait()


def per_device(latent, w_in, output_weight, targets, area_weights, live_counts):
    vmem = pl.BlockSpec(memory_space=pltpu.VMEM)
    hbm = pl.BlockSpec(memory_space=pl.ANY)
    V = pltpu.VMEM
    dma = pltpu.SemaphoreType.DMA
    widths = [p[2] for p in PIECES]
    scratch = [
        V((2, POINTS, FEATURES), BF16),
        V((2, CHUNK, FEATURES), F32),
        V((FEATURES, FEATURES), BF16),
        V((VARS, FEATURES), BF16),
        V((VARS, POINTS), BF16),
        V((8, LANES), F32),
        V((2, POINTS, FEATURES), BF16),
        V((2, POINTS, FEATURES), BF16),
        V((2, 16, 2, ROWS, HALF), F32),
        V((CHUNKS, 4, 2, VARS, LANES), BF16),
        V((CHUNKS, 4, 2, VARS, LANES), BF16),
        V((CHUNKS, 4, 2, VARS, LANES), BF16),
        V((CHUNKS, 4, 2, VARS, LANES), BF16),
        V((VARS, FEATURES), F32),
        V((2, 16, ROWS, HALF), BF16),
        V((2, 16, ROWS, HALF), BF16),
        [V((4, 4, ROWS, n), BF16) for n in widths],
        [V((3, 4, ROWS, n), BF16) for n in widths],
        [V((4, ROWS, n), BF16) for n in widths],
        [V((3, ROWS, n), BF16) for n in widths],
        [V((4, ROWS, 2 * widths[0]), BF16), V((4, ROWS, 2 * widths[2]), BF16)],
        V((4, 16, 16, LANES), BF16),
        V((3, 16, 16, LANES), BF16),
        V((4, 4, 16, LANES), BF16),
        V((3, 4, 16, LANES), BF16),
        V((4, 16, LANES), BF16),
        V((16, 16, LANES), BF16),
        V((4, VARS, LANES), BF16),
        V((4, VARS, LANES), BF16),
        V((4, VARS, LANES), BF16),
        V((3, VARS, LANES), BF16),
        V((4, VARS, LANES), BF16),
        V((4, VARS, LANES), BF16),
        V((8, VARS, LANES), BF16),
        V((8, 8, LANES), F32),
        V((4, 8, LANES), F32),
        V((2, 8, LANES), F32),
        V((4, 8, LANES), F32),
        V((4, 8, LANES), F32),
        V((4, 8, LANES), F32),
        dma((11,)),
        dma((SENDS,)),
        dma((CHUNKS, 2)),
        dma((CHUNKS,)),
        dma((15,)),
        dma((5,)),
        dma((6,)),
    ]
    operands = (latent, w_in, output_weight, targets, area_weights.reshape(8, LANES))
    results = pl.pallas_call(
        kernel,
        out_shape=[
            V((8, LANES), F32),
            V(latent.shape, BF16),
            V((ROWS, FEATURES), F32),
            V((VARS, FEATURES), F32),
        ],
        in_specs=[pl.BlockSpec(memory_space=pltpu.HBM)] * 5 + [pl.BlockSpec(memory_space=pltpu.SMEM)],
        out_specs=[vmem] * 4,
        scratch_shapes=scratch,
        compiler_params=pltpu.CompilerParams(collective_id=1, has_side_effects=True, vmem_limit_bytes=48 << 20),
        name="energy_step",
    )(*[pltpu.with_memory_space_constraint(a, pltpu.HBM) for a in operands], live_counts)
    loss, glat, gwin, gwout = pl.pallas_call(
        write_out,
        out_shape=[
            jax.ShapeDtypeStruct((1, 1), F32),
            jax.ShapeDtypeStruct(latent.shape, BF16),
            jax.ShapeDtypeStruct((ROWS, FEATURES), F32),
            jax.ShapeDtypeStruct((VARS, FEATURES), F32),
        ],
        in_specs=[vmem] * 4,
        out_specs=[vmem] + [hbm] * 3,
        scratch_shapes=[dma((3,))],
        compiler_params=pltpu.CompilerParams(vmem_limit_bytes=1 << 20),
        name="write_out",
    )(*[pltpu.with_memory_space_constraint(r, pltpu.VMEM) for r in results])
    return loss.reshape(()), glat, gwin, gwout


def solution(mesh):
    placed = (P("ens", "sp", None), P(), P(), P(None, "sp"), P("sp"), P("sp"))
    return jax.shard_map(
        per_device,
        mesh=mesh,
        in_specs=placed,
        out_specs=(P(), P("ens", "sp", None), P("sp", None), P()),
        check_vma=False,
    )
```

```python
import functools
import math

import jax
import jax.numpy as jnp
from jax import lax
from jax.experimental import pallas as pl
from jax.experimental.pallas import tpu as pltpu
from jax.sharding import PartitionSpec as P

BF16, F32 = jnp.bfloat16, jnp.float32
MESH = pl.DeviceIdType.MESH
LOSS_SCALE = 1024.0
MEMBERS, VARS, FEATURES, POINTS = 8, 80, 1024, 1024
CHUNKS = 2
CHUNK = POINTS // CHUNKS
LANES = 128
HALF = FEATURES // 2
PIECES = ((0, 256, 128, "y"), (0, 384, 128, "z"), (1, 0, 256, "y"), (1, 256, 256, "z"))
SENDS = 8
FAR = ((2, 2), (2, 1), (2, 3), (1, 2), (3, 2))
ROWS = 32
OUTER = math.sqrt(2.0 / math.pi)
INNER = OUTER * 0.044715


def dot(a, b, ca, cb):
    return lax.dot_general(a, b, (((ca,), (cb,)), ((), ())), preferred_element_type=F32)


def activation(z):
    cubic = INNER * (z * z)
    s = 0.5 * jnp.tanh(z * (cubic + OUTER)) + 0.5
    h = z * s
    slope = s + (h - h * s) * (6.0 * cubic + 2.0 * OUTER)
    return h.astype(BF16), slope.astype(BF16)


def activation_only(z):
    return (z * (0.5 * jnp.tanh(z * (INNER * (z * z) + OUTER)) + 0.5)).astype(BF16)


def score_block(x_ref, y, weighted, store):
    n = MEMBERS
    pairs = [(i, j) for i in range(n) for j in range(i + 1, n)]
    step = 16
    own = [jnp.zeros((step, LANES), F32) for _ in range(n)]
    between = [jnp.zeros((step, LANES), F32) for _ in pairs]
    for v in range(0, VARS, step):
        x = [x_ref[m // 2, m % 2, v : v + step, :].astype(F32) for m in range(n)]
        for m in range(n):
            d = x[m] - y[v : v + step]
            own[m] = own[m] + d * d
        for q, (i, j) in enumerate(pairs):
            d = x[i] - x[j]
            between[q] = between[q] + d * d
    a = [jnp.sqrt(jnp.sum(o, axis=0, keepdims=True) + 1.0) for o in own]
    b = [jnp.sqrt(jnp.sum(o, axis=0, keepdims=True) + 1.0) for o in between]
    score = sum(a) / n - sum(b) / (n * (n - 1.0))
    from_target = [weighted / (n * t) for t in a]
    from_pair = [weighted / (n * (n - 1.0) * t) for t in b]
    for v in range(0, VARS, step):
        x = [x_ref[m // 2, m % 2, v : v + step, :].astype(F32) for m in range(n)]
        total = [(x[m] - y[v : v + step]) * from_target[m] for m in range(n)]
        for q, (i, j) in enumerate(pairs):
            d = (x[i] - x[j]) * from_pair[q]
            total[i] = total[i] - d
            total[j] = total[j] + d
        for m in range(n):
            store(m, v, step, total[m].astype(BF16))
    return weighted * score


def kernel(
    lat_hbm, w_hbm, wout_hbm, targets_hbm, area_hbm, live,
    loss_out, glat_out, gwin_out, gwout_out,
    lat, later, w, wout, targets, area, hid, back, acc, fsend, frecv, ssend, srecv, gout,
    core_send, core_recv, one_send, one_recv, two_send, two_recv, three,
    x_send, x_recv, xy_send, xy_recv, xz_send, x_all,
    g_core_send, g_core_recv, g_one_send, g_one_recv, g_two, g_three, g_all,
    ls_core, ls_y, ls_z, ls_x,
    in_sem, out_sem, f_rs, s_rs, p_rs, g_rs, t_rs,
):
    e = lax.axis_index("ens")
    sp = lax.axis_index("sp")
    core = lax.rem(sp, 2)
    z = lax.rem(sp // 2, 4)
    y = sp // 8

    def turn(i, d):
        return lax.rem(i + d, 4)

    def device(x_, y_, z_, core_):
        return (x_, (y_ * 4 + z_) * 2 + core_)

    along = {
        "x": lambda d: device(turn(e, d), y, z, core),
        "y": lambda d: device(e, turn(y, d), z, core),
        "z": lambda d: device(e, y, turn(z, d), core),
    }
    place = {"x": e, "y": y, "z": z}
    sibling = device(e, y, z, 1 - core)

    def load(m, c):
        s = pl.ds(c * CHUNK, CHUNK)
        return pltpu.make_async_copy(lat_hbm.at[m, s], lat.at[m, s], in_sem.at[2 * c + m])

    loads = {(c, m): load(m, c) for c in range(CHUNKS) for m in range(2)}
    small = [
        pltpu.make_async_copy(src, dst, in_sem.at[8 + i])
        for i, (src, dst) in enumerate([(area_hbm, area), (wout_hbm, wout), (targets_hbm, targets)])
    ]
    loads[0, 0].start()
    load_w = []
    for i in range(2):
        cols = pl.ds(i * HALF, HALF)
        load_w.append(pltpu.make_async_copy(w_hbm.at[:, cols], w.at[:, cols], in_sem.at[4 + i]))
        load_w[i].start()
    for cp in small:
        cp.start()

    peers = [along[k](d) for k in "xyz" for d in (1, 2, 3)] + [sibling]
    peers += [device(turn(e, dx), y, turn(z, dz), core) for dx in (1, 2, 3) for dz in (1, 2, 3)]
    barrier = pltpu.get_barrier_semaphore()
    for p in peers:
        pl.semaphore_signal(barrier, inc=1, device_id=p, device_id_type=MESH)

    def remote(src, dst, ss, rs, to):
        return pltpu.make_async_remote_copy(
            src_ref=src, dst_ref=dst, send_sem=ss, recv_sem=rs, device_id=to, device_id_type=MESH
        )

    leaving = {}
    turns = [0]

    def send(copies, rs, whole, sent=None):
        k = turns[0] % SENDS
        turns[0] += 1
        if k in leaving:
            leaving.pop(k)()
        ss = out_sem.at[k]
        for src, dst, to in copies:
            remote(src, dst, ss, rs, to).start()
        sent = whole if sent is None else sent
        leaving[k] = lambda: remote(sent, sent, ss, rs, sibling).wait_send()
        return lambda: remote(whole, whole, ss, rs, sibling).wait_recv()

    def spread(axis, src, dst, rs, whole, sent=None, hops=(2, 1, 3)):
        own = place[axis]
        return send([(src(turn(own, d)), dst(d, own), along[axis](d)) for d in hops], rs, whole, sent)

    def share(axis, buf, rs):
        return spread(axis, lambda k: buf.at[place[axis]], lambda d, own: buf.at[own], rs, buf.at[pl.ds(0, 3)])

    def four(ref):
        return (ref[0].astype(F32) + ref[1].astype(F32)) + (ref[2].astype(F32) + ref[3].astype(F32))

    def received(own, ref):
        total = own.astype(F32)
        for d in range(3):
            total = total + ref[d].astype(F32)
        return total

    def sums_tile(scores):
        where = lax.broadcasted_iota(jnp.int32, (8, LANES), 0) * LANES + lax.broadcasted_iota(jnp.int32, (8, LANES), 1)
        is_live = (where < live[0]).astype(F32)
        row = lax.broadcasted_iota(jnp.int32, (8, LANES), 0)
        weights = jnp.sum(area[...] * is_live, axis=0, keepdims=True)
        return jnp.where(row == 0, scores, jnp.where(row == 1, weights, jnp.sum(is_live, axis=0, keepdims=True)))

    def slopes_of_gelu(c, m):
        s = pl.ds(c * CHUNK, CHUNK)
        back[m, s, :] = activation(later[m, s, :])[1]

    def forecast(c, m):
        f = dot(wout[...], hid[m, c * CHUNK : (c + 1) * CHUNK, :], 1, 1).astype(BF16)
        for k in range(4):
            fsend[c, k, m] = f[:, k * LANES : (k + 1) * LANES]
        frecv[c, e, m] = fsend[c, e, m]

    def forward(c, m):
        s = pl.ds(c * CHUNK, CHUNK)
        pre = jnp.dot(lat[m, s, :], w[...], preferred_element_type=F32)
        hid[m, s, :] = activation_only(pre)
        later[m, s, :] = pre
        forecast(c, m)

    def forward_send(c, m, hops=(2, 1, 3)):
        return spread(
            "x", lambda k: fsend.at[c, k, m], lambda d, own: frecv.at[c, own, m], f_rs.at[c, m],
            frecv.at[c, pl.ds(0, 3), m], frecv.at[c, pl.ds(0, len(hops)), m], hops,
        )

    def forward_half(c, m, hops):
        rows = [pl.ds(pl.multiple_of(c * CHUNK + turn(e, d) * LANES, LANES), LANES) for d in hops]
        pre = jnp.dot(
            jnp.concatenate([lat[m, r, :] for r in rows], axis=0), w[...], preferred_element_type=F32
        )
        h = activation_only(pre)
        for i, r in enumerate(rows):
            hid[m, r, :] = h[i * LANES : (i + 1) * LANES]
            later[m, r, :] = pre[i * LANES : (i + 1) * LANES]
        f = dot(wout[...], h, 1, 1).astype(BF16)
        for i, d in enumerate(hops):
            fsend[c, turn(e, d), m] = f[:, i * LANES : (i + 1) * LANES]

    def scored(c):
        block = c * 4 + e
        y_block = targets[:, pl.ds(pl.multiple_of(block * LANES, LANES), LANES)].astype(F32)
        lanes = lax.broadcasted_iota(jnp.int32, (1, LANES), 1)
        weighted = area[pl.ds(block, 1), :] * (block * LANES + lanes < live[0]).astype(F32)

        def store(m, v, step, value):
            ssend[c, m // 2, m % 2, v : v + step, :] = value

        row = score_block(frecv.at[c], y_block, weighted, store)
        srecv[c, e] = ssend[c, e]
        return row

    def scored_send(c):
        return spread(
            "x", lambda k: ssend.at[c, k], lambda d, own: srecv.at[c, own], s_rs.at[c], srecv.at[c, pl.ds(0, 3)]
        )

    def backward(c, lo, wide):
        s, cols = pl.ds(c * CHUNK, CHUNK), slice(lo, lo + wide)
        for m in range(2):
            slopes = jnp.concatenate([srecv[c, k, m] for k in range(4)], axis=1)
            bh = dot(slopes, wout[:, cols], 0, 0)
            back[m, s, cols] = (back[m, s, cols].astype(F32) * bh).astype(BF16)

    def output_part(c):
        s = pl.ds(c * CHUNK, CHUNK)
        slopes = jnp.concatenate([srecv[c, k, m] for m in range(2) for k in range(4)], axis=1)
        return dot(slopes, hid[:, s, :].reshape(2 * CHUNK, FEATURES), 1, 0)

    def weight_early():
        a = lat[:, :CHUNK, :].reshape(2 * CHUNK, FEATURES)
        term = dot(a, back[:, :CHUNK, :].reshape(2 * CHUNK, FEATURES), 0, 0)
        for i in range(2):
            acc[i] = term[:, i * HALF : (i + 1) * HALF].reshape(16, 2, ROWS, HALF)

    def weight_half(i):
        cols = slice(i * HALF, (i + 1) * HALF)
        a = lat[:, CHUNK:, :].reshape(2 * CHUNK, FEATURES)
        acc[i] += dot(a, back[:, CHUNK:, cols].reshape(2 * CHUNK, HALF), 0, 0).reshape(16, 2, ROWS, HALF)

    def g_start():
        def body(k, _):
            cols = pl.ds(pl.multiple_of((k * 2 + 1 - core) * LANES, LANES), LANES)
            g_core_send[k] = gout[:, cols].astype(BF16)
            return 0

        lax.fori_loop(0, 4, body, 0)
        return send([(g_core_send, g_core_recv, sibling)], g_rs.at[0], g_core_recv)

    def g_to_first(arrived):
        arrived()

        def body(k, _):
            cols = pl.ds(pl.multiple_of((k * 2 + core) * LANES, LANES), LANES)
            g_one_send[k] = (gout[:, cols] + g_core_recv[k].astype(F32)).astype(BF16)
            return 0

        lax.fori_loop(0, 4, body, 0)
        return spread("y", lambda k: g_one_send.at[k], lambda d, own: g_one_recv.at[d - 1], g_rs.at[1], g_one_recv)

    def g_to_second(arrived):
        arrived()
        g_two[e] = received(g_one_send[y], g_one_recv).astype(BF16)
        return share("x", g_two, g_rs.at[2])

    def g_to_third(arrived):
        arrived()
        g_three[z] = four(g_two).astype(BF16)
        return share("z", g_three, g_rs.at[3])

    def g_to_all(arrived, share_of):
        arrived()
        g_all[core, y] = (four(g_three) * share_of).astype(BF16)
        return spread("y", lambda k: g_all.at[core, y], lambda d, own: g_all.at[core, own], g_rs.at[4], g_all.at[0, pl.ds(0, 3)])

    def g_to_sibling(arrived):
        arrived()
        return send([(g_all.at[core], g_all.at[core], sibling)], g_rs.at[5], g_all.at[0])

    def g_finish(arrived):
        arrived()
        for k in range(8):
            gwout_out[:, k * LANES : (k + 1) * LANES] = g_all[k % 2, k // 2].astype(F32)

    def to_core(i):
        core_send[i] = acc[i, :, 1 - core].astype(BF16)
        return send([(core_send.at[i], core_recv.at[i], sibling)], p_rs.at[i], core_recv.at[i])

    def from_core(i, lo, wide):
        cols = slice(lo, lo + wide)
        return (acc[i, :, core, :, cols] + core_recv[i, :, :, cols].astype(F32)).astype(BF16)

    def part(j, k):
        return one_send[j].at[k] if PIECES[j][3] == "y" else one_send[j].at[:, k]

    def to_first(j):
        half, lo, wide, axis = PIECES[j]
        one_send[j][...] = from_core(half, lo, wide).reshape(4, 4, ROWS, wide)
        return spread(
            axis, lambda k: part(j, k), lambda d, own: one_recv[j].at[d - 1], p_rs.at[2 + j], one_recv[j]
        )

    def to_second(j, arrived):
        arrived()
        axis = PIECES[j][3]
        two_send[j][...] = received(part(j, place[axis])[...], one_recv[j]).astype(BF16)
        return spread(
            "z" if axis == "y" else "y", lambda k: two_send[j].at[k], lambda d, own: two_recv[j].at[d - 1],
            p_rs.at[6 + j], two_recv[j],
        )

    def to_third(i, arrived):
        for j in (2 * i, 2 * i + 1):
            arrived[j]()
            wide, own = PIECES[j][2], place["z" if PIECES[j][3] == "y" else "y"]
            lo = (j % 2) * wide
            three[i][e, :, lo : lo + wide] = received(two_send[j][own], two_recv[j]).astype(BF16)
        return share("x", three[i], p_rs.at[10 + i])

    def finish(i, arrived, share_of):
        arrived()
        wide = 2 * PIECES[2 * i][2]
        gwin_out[:, FEATURES // 4 * (1 + i) : FEATURES // 4 * (1 + i) + wide] = four(three[i]) * share_of

    def x_block(k):
        return slice((k // 2) * 16, (k // 2 + 1) * 16), slice((k % 2) * LANES, (k % 2 + 1) * LANES)

    def x_first():
        total = from_core(0, 0, 2 * LANES)
        for k in range(4):
            rows, cols = x_block(k)
            x_send[k] = total[:, rows, cols]
        return spread("x", lambda k: x_send.at[k], lambda d, own: x_recv.at[d - 1], p_rs.at[12], x_recv)

    def x_second(arrived):
        arrived()
        xy_send[...] = received(x_send[e], x_recv).astype(BF16).reshape(4, 4, 16, LANES)
        return spread("y", lambda k: xy_send.at[k], lambda d, own: xy_recv.at[d - 1], p_rs.at[13], xy_recv)

    def x_third(arrived):
        arrived()
        xz_send[...] = received(xy_send[y], xy_recv).astype(BF16)
        slot = e * 4 + z
        x_all[slot] = xz_send[z]
        copies = []
        for dx, dz in sorted(((i, j) for i in range(4) for j in range(4) if i or j), key=lambda h: h not in FAR):
            to = turn(z, dz)
            copies.append((xz_send.at[to], x_all.at[slot], device(turn(e, dx), y, to, core)))
        return send(copies, p_rs.at[14], x_all.at[pl.ds(0, 15)])

    def x_finish(arrived, share_of):
        arrived()
        for k in range(4):
            rows, cols = x_block(k)
            gwin_out[rows, cols] = four(x_all.at[pl.ds(4 * k, 4)]) * share_of

    def latent_tile(i, factor):
        m, s = i // 2, pl.ds((i % 2) * CHUNK, CHUNK)
        glat_out[m, s, :] = (dot(back[m, s, :], w[...], 1, 1) * factor).astype(BF16)

    loads[0, 0].wait()
    load_w[0].wait()
    loads[0, 1].start()
    for i in range(2):
        cols = slice(i * HALF, (i + 1) * HALF)
        if i == 1:
            load_w[1].wait()
            loads[1, 0].start()
            loads[1, 1].start()
        pre00 = jnp.dot(lat[0, :CHUNK, :], w[:, cols], preferred_element_type=F32)
        hid[0, :CHUNK, cols], back[0, :CHUNK, cols] = activation(pre00)
    small[1].wait()
    forecast(0, 0)
    pl.semaphore_wait(barrier, len(peers))
    f00 = forward_send(0, 0)
    loads[0, 1].wait()
    forward(0, 1)
    f01 = forward_send(0, 1)
    loads[1, 0].wait()
    forward(1, 0)
    f10 = forward_send(1, 0)
    loads[1, 1].wait()
    forward_half(1, 1, (2, 1))
    f11 = forward_send(1, 1, (2, 1))
    f00()
    f01()
    small[0].wait()
    small[2].wait()
    row0 = scored(0)
    s0 = scored_send(0)
    forward_half(1, 1, (3, 0))
    forward_send(1, 1, (3,))
    frecv[1, e, 1] = fsend[1, e, 1]
    slopes_of_gelu(0, 1)
    slopes_of_gelu(1, 0)
    slopes_of_gelu(1, 1)
    f10()
    f11()
    row1 = scored(1)
    s1 = scored_send(1)
    ls_core[core] = sums_tile(row0 + row1)
    lc = send([(ls_core.at[core], ls_core.at[core], sibling)], t_rs.at[0], ls_core.at[0])
    s0()
    backward(0, 0, FEATURES)
    gout[...] = output_part(0)
    lc()
    ls_y[y] = ls_core[0] + ls_core[1]
    lc = share("y", ls_y, t_rs.at[1])
    weight_early()
    s1()
    gout[...] += output_part(1)
    g = g_start()
    lc()
    ls_z[z] = four(ls_y)
    lc = share("z", ls_z, t_rs.at[2])
    backward(1, 0, HALF)
    weight_half(0)
    c0 = to_core(0)
    g = g_to_first(g)
    backward(1, HALF, HALF)
    weight_half(1)
    c1 = to_core(1)
    c0()
    p = {}
    xf = x_first()
    p[0] = to_first(0)
    p[1] = to_first(1)
    lc()
    sums = four(ls_z)
    ls_x[e] = sums
    lc = share("x", ls_x, t_rs.at[3])
    totals = jnp.sum(sums, axis=1, keepdims=True)
    weight_total, live_total = totals[1:2, 0:1], totals[2:3, 0:1]
    factor = LOSS_SCALE * live_total / weight_total
    latent_tile(0, factor)
    g = g_to_second(g)
    c1()
    p[2] = to_first(2)
    p[3] = to_first(3)
    latent_tile(1, factor)
    latent_tile(2, factor)
    xf = x_second(xf)
    p[0] = to_second(0, p[0])
    p[1] = to_second(1, p[1])
    g = g_to_third(g)
    latent_tile(3, factor)
    lc()
    loss_out[...] = jnp.sum(four(ls_x), axis=1, keepdims=True) / weight_total + jnp.zeros((8, LANES), F32)
    share_of = LOSS_SCALE / weight_total
    p[2] = to_second(2, p[2])
    p[3] = to_second(3, p[3])
    xf = x_third(xf)
    xa = to_third(0, p)
    g = g_to_all(g, share_of)
    xb = to_third(1, p)
    finish(0, xa, share_of)
    g = g_to_sibling(g)
    x_finish(xf, share_of)
    g_finish(g)
    finish(1, xb, share_of)
    for left in leaving.values():
        left()


def write_out(loss, glat, gwin, gwout, loss_out, glat_out, gwin_out, gwout_out, sem):
    pairs = [(glat, glat_out), (gwin, gwin_out), (gwout, gwout_out)]
    cps = [pltpu.make_async_copy(src, dst, sem.at[i]) for i, (src, dst) in enumerate(pairs)]
    for cp in cps:
        cp.start()
    loss_out[...] = loss[0:1, 0:1]
    for cp in cps:
        cp.wait()


def per_device(latent, w_in, output_weight, targets, area_weights, live_counts):
    vmem = pl.BlockSpec(memory_space=pltpu.VMEM)
    hbm = pl.BlockSpec(memory_space=pl.ANY)
    V = pltpu.VMEM
    dma = pltpu.SemaphoreType.DMA
    widths = [p[2] for p in PIECES]
    scratch = [
        V((2, POINTS, FEATURES), BF16),
        V((2, POINTS, FEATURES), F32),
        V((FEATURES, FEATURES), BF16),
        V((VARS, FEATURES), BF16),
        V((VARS, POINTS), BF16),
        V((8, LANES), F32),
        V((2, POINTS, FEATURES), BF16),
        V((2, POINTS, FEATURES), BF16),
        V((2, 16, 2, ROWS, HALF), F32),
        V((CHUNKS, 4, 2, VARS, LANES), BF16),
        V((CHUNKS, 4, 2, VARS, LANES), BF16),
        V((CHUNKS, 4, 2, VARS, LANES), BF16),
        V((CHUNKS, 4, 2, VARS, LANES), BF16),
        V((VARS, FEATURES), F32),
        V((2, 16, ROWS, HALF), BF16),
        V((2, 16, ROWS, HALF), BF16),
        [V((4, 4, ROWS, n), BF16) for n in widths],
        [V((3, 4, ROWS, n), BF16) for n in widths],
        [V((4, ROWS, n), BF16) for n in widths],
        [V((3, ROWS, n), BF16) for n in widths],
        [V((4, ROWS, 2 * widths[0]), BF16), V((4, ROWS, 2 * widths[2]), BF16)],
        V((4, 16, 16, LANES), BF16),
        V((3, 16, 16, LANES), BF16),
        V((4, 4, 16, LANES), BF16),
        V((3, 4, 16, LANES), BF16),
        V((4, 16, LANES), BF16),
        V((16, 16, LANES), BF16),
        V((4, VARS, LANES), BF16),
        V((4, VARS, LANES), BF16),
        V((4, VARS, LANES), BF16),
        V((3, VARS, LANES), BF16),
        V((4, VARS, LANES), BF16),
        V((4, VARS, LANES), BF16),
        V((2, 4, VARS, LANES), BF16),
        V((2, 8, LANES), F32),
        V((4, 8, LANES), F32),
        V((4, 8, LANES), F32),
        V((4, 8, LANES), F32),
        dma((11,)),
        dma((SENDS,)),
        dma((CHUNKS, 2)),
        dma((CHUNKS,)),
        dma((15,)),
        dma((6,)),
        dma((4,)),
    ]
    operands = (latent, w_in, output_weight, targets, area_weights.reshape(8, LANES))
    results = pl.pallas_call(
        kernel,
        out_shape=[
            V((8, LANES), F32),
            V(latent.shape, BF16),
            V((ROWS, FEATURES), F32),
            V((VARS, FEATURES), F32),
        ],
        in_specs=[pl.BlockSpec(memory_space=pltpu.HBM)] * 5 + [pl.BlockSpec(memory_space=pltpu.SMEM)],
        out_specs=[vmem] * 4,
        scratch_shapes=scratch,
        compiler_params=pltpu.CompilerParams(collective_id=1, has_side_effects=True, vmem_limit_bytes=48 << 20),
        name="energy_step",
    )(*[pltpu.with_memory_space_constraint(a, pltpu.HBM) for a in operands], live_counts)
    loss, glat, gwin, gwout = pl.pallas_call(
        write_out,
        out_shape=[
            jax.ShapeDtypeStruct((1, 1), F32),
            jax.ShapeDtypeStruct(latent.shape, BF16),
            jax.ShapeDtypeStruct((ROWS, FEATURES), F32),
            jax.ShapeDtypeStruct((VARS, FEATURES), F32),
        ],
        in_specs=[vmem] * 4,
        out_specs=[vmem] + [hbm] * 3,
        scratch_shapes=[dma((3,))],
        compiler_params=pltpu.CompilerParams(vmem_limit_bytes=1 << 20),
        name="write_out",
    )(*[pltpu.with_memory_space_constraint(r, pltpu.VMEM) for r in results])
    return loss.reshape(()), glat, gwin, gwout


def solution(mesh):
    placed = (P("ens", "sp", None), P(), P(), P(None, "sp"), P("sp"), P("sp"))
    return jax.shard_map(
        per_device,
        mesh=mesh,
        in_specs=placed,
        out_specs=(P(), P("ens", "sp", None), P("sp", None), P()),
        check_vma=False,
    )
```

```python
import functools
import math

import jax
import jax.numpy as jnp
from jax import lax
from jax.experimental import pallas as pl
from jax.experimental.pallas import tpu as pltpu
from jax.sharding import PartitionSpec as P

BF16, F32 = jnp.bfloat16, jnp.float32
MESH = pl.DeviceIdType.MESH
LOSS_SCALE = 1024.0
MEMBERS, VARS, FEATURES, POINTS = 8, 80, 1024, 1024
CHUNKS = 2
CHUNK = POINTS // CHUNKS
LANES = 128
HALF = FEATURES // 2
PIECES = ((0, 256, 128, "y"), (0, 384, 128, "z"), (1, 0, 256, "y"), (1, 256, 256, "z"))
SENDS = 8
FAR = ((2, 2), (2, 1), (2, 3), (1, 2), (3, 2))
ROWS = 32
OUTER = math.sqrt(2.0 / math.pi)
INNER = OUTER * 0.044715


def dot(a, b, ca, cb):
    return lax.dot_general(a, b, (((ca,), (cb,)), ((), ())), preferred_element_type=F32)


def activation(z):
    cubic = INNER * (z * z)
    s = 0.5 * jnp.tanh(z * (cubic + OUTER)) + 0.5
    h = z * s
    slope = s + (h - h * s) * (6.0 * cubic + 2.0 * OUTER)
    return h.astype(BF16), slope.astype(BF16)


def activation_only(z):
    return (z * (0.5 * jnp.tanh(z * (INNER * (z * z) + OUTER)) + 0.5)).astype(BF16)


def score_block(x_ref, y, weighted, store):
    n = MEMBERS
    pairs = [(i, j) for i in range(n) for j in range(i + 1, n)]
    step = 16
    own = [jnp.zeros((step, LANES), F32) for _ in range(n)]
    between = [jnp.zeros((step, LANES), F32) for _ in pairs]
    for v in range(0, VARS, step):
        x = [x_ref[m // 2, m % 2, v : v + step, :].astype(F32) for m in range(n)]
        for m in range(n):
            d = x[m] - y[v : v + step]
            own[m] = own[m] + d * d
        for q, (i, j) in enumerate(pairs):
            d = x[i] - x[j]
            between[q] = between[q] + d * d
    a = [jnp.sqrt(jnp.sum(o, axis=0, keepdims=True) + 1.0) for o in own]
    b = [jnp.sqrt(jnp.sum(o, axis=0, keepdims=True) + 1.0) for o in between]
    score = sum(a) / n - sum(b) / (n * (n - 1.0))
    from_target = [weighted / (n * t) for t in a]
    from_pair = [weighted / (n * (n - 1.0) * t) for t in b]
    for v in range(0, VARS, step):
        x = [x_ref[m // 2, m % 2, v : v + step, :].astype(F32) for m in range(n)]
        total = [(x[m] - y[v : v + step]) * from_target[m] for m in range(n)]
        for q, (i, j) in enumerate(pairs):
            d = (x[i] - x[j]) * from_pair[q]
            total[i] = total[i] - d
            total[j] = total[j] + d
        for m in range(n):
            store(m, v, step, total[m].astype(BF16))
    return weighted * score


def kernel(
    lat_hbm, w_hbm, wout_hbm, targets_hbm, area_hbm, live,
    loss_out, glat_out, gwin_out, gwout_out,
    lat, later, w, wout, targets, area, hid, back, acc, fsend, frecv, ssend, srecv, gout,
    core_send, core_recv, one_send, one_recv, two_send, two_recv, three,
    x_send, x_recv, xy_send, xy_recv, xz_send, x_all,
    g_core_send, g_core_recv, g_one_send, g_one_recv, g_two, g_three, g_all,
    ls_core, ls_y, ls_z, ls_x,
    in_sem, out_sem, f_rs, s_rs, p_rs, g_rs, t_rs,
):
    e = lax.axis_index("ens")
    sp = lax.axis_index("sp")
    core = lax.rem(sp, 2)
    z = lax.rem(sp // 2, 4)
    y = sp // 8

    def turn(i, d):
        return lax.rem(i + d, 4)

    def device(x_, y_, z_, core_):
        return (x_, (y_ * 4 + z_) * 2 + core_)

    along = {
        "x": lambda d: device(turn(e, d), y, z, core),
        "y": lambda d: device(e, turn(y, d), z, core),
        "z": lambda d: device(e, y, turn(z, d), core),
    }
    place = {"x": e, "y": y, "z": z}
    sibling = device(e, y, z, 1 - core)

    def load(m, c):
        s = pl.ds(c * CHUNK, CHUNK)
        return pltpu.make_async_copy(lat_hbm.at[m, s], lat.at[m, s], in_sem.at[2 * c + m])

    loads = {(c, m): load(m, c) for c in range(CHUNKS) for m in range(2)}
    small = [
        pltpu.make_async_copy(src, dst, in_sem.at[8 + i])
        for i, (src, dst) in enumerate([(area_hbm, area), (wout_hbm, wout), (targets_hbm, targets)])
    ]
    loads[0, 0].start()
    load_w = []
    for i in range(2):
        cols = pl.ds(i * HALF, HALF)
        load_w.append(pltpu.make_async_copy(w_hbm.at[:, cols], w.at[:, cols], in_sem.at[4 + i]))
        load_w[i].start()
    for cp in small:
        cp.start()

    peers = [along[k](d) for k in "xyz" for d in (1, 2, 3)] + [sibling]
    peers += [device(turn(e, dx), y, turn(z, dz), core) for dx in (1, 2, 3) for dz in (1, 2, 3)]
    barrier = pltpu.get_barrier_semaphore()
    for p in peers:
        pl.semaphore_signal(barrier, inc=1, device_id=p, device_id_type=MESH)

    def remote(src, dst, ss, rs, to):
        return pltpu.make_async_remote_copy(
            src_ref=src, dst_ref=dst, send_sem=ss, recv_sem=rs, device_id=to, device_id_type=MESH
        )

    leaving = {}
    turns = [0]

    def send(copies, rs, whole, sent=None):
        k = turns[0] % SENDS
        turns[0] += 1
        if k in leaving:
            leaving.pop(k)()
        ss = out_sem.at[k]
        for src, dst, to in copies:
            remote(src, dst, ss, rs, to).start()
        sent = whole if sent is None else sent
        leaving[k] = lambda: remote(sent, sent, ss, rs, sibling).wait_send()
        return lambda: remote(whole, whole, ss, rs, sibling).wait_recv()

    def spread(axis, src, dst, rs, whole, sent=None, hops=(2, 1, 3)):
        own = place[axis]
        return send([(src(turn(own, d)), dst(d, own), along[axis](d)) for d in hops], rs, whole, sent)

    def share(axis, buf, rs):
        return spread(axis, lambda k: buf.at[place[axis]], lambda d, own: buf.at[own], rs, buf.at[pl.ds(0, 3)])

    def four(ref):
        return (ref[0].astype(F32) + ref[1].astype(F32)) + (ref[2].astype(F32) + ref[3].astype(F32))

    def received(own, ref):
        total = own.astype(F32)
        for d in range(3):
            total = total + ref[d].astype(F32)
        return total

    def sums_tile(scores):
        where = lax.broadcasted_iota(jnp.int32, (8, LANES), 0) * LANES + lax.broadcasted_iota(jnp.int32, (8, LANES), 1)
        is_live = (where < live[0]).astype(F32)
        row = lax.broadcasted_iota(jnp.int32, (8, LANES), 0)
        weights = jnp.sum(area[...] * is_live, axis=0, keepdims=True)
        return jnp.where(row == 0, scores, jnp.where(row == 1, weights, jnp.sum(is_live, axis=0, keepdims=True)))

    def slopes_of_gelu(c, m):
        s = pl.ds(c * CHUNK, CHUNK)
        back[m, s, :] = activation(later[m, s, :])[1]

    def forecast(c, m):
        f = dot(wout[...], hid[m, c * CHUNK : (c + 1) * CHUNK, :], 1, 1).astype(BF16)
        for k in range(4):
            fsend[c, k, m] = f[:, k * LANES : (k + 1) * LANES]
        frecv[c, e, m] = fsend[c, e, m]

    def forward(c, m):
        s = pl.ds(c * CHUNK, CHUNK)
        pre = jnp.dot(lat[m, s, :], w[...], preferred_element_type=F32)
        hid[m, s, :] = activation_only(pre)
        later[m, s, :] = pre
        forecast(c, m)

    def forward_first(cols):
        pre = jnp.dot(lat[0, :CHUNK, :], w[:, cols], preferred_element_type=F32)
        hid[0, :CHUNK, cols], back[0, :CHUNK, cols] = activation(pre)

    def forward_send(c, m, hops=(2, 1, 3)):
        return spread(
            "x", lambda k: fsend.at[c, k, m], lambda d, own: frecv.at[c, own, m], f_rs.at[c, m],
            frecv.at[c, pl.ds(0, 3), m], frecv.at[c, pl.ds(0, len(hops)), m], hops,
        )

    def forward_half(c, m, hops):
        rows = [pl.ds(pl.multiple_of(c * CHUNK + turn(e, d) * LANES, LANES), LANES) for d in hops]
        pre = jnp.dot(
            jnp.concatenate([lat[m, r, :] for r in rows], axis=0), w[...], preferred_element_type=F32
        )
        h = activation_only(pre)
        for i, r in enumerate(rows):
            hid[m, r, :] = h[i * LANES : (i + 1) * LANES]
            later[m, r, :] = pre[i * LANES : (i + 1) * LANES]
        f = dot(wout[...], h, 1, 1).astype(BF16)
        for i, d in enumerate(hops):
            fsend[c, turn(e, d), m] = f[:, i * LANES : (i + 1) * LANES]

    def scored(c):
        block = c * 4 + e
        y_block = targets[:, pl.ds(pl.multiple_of(block * LANES, LANES), LANES)].astype(F32)
        lanes = lax.broadcasted_iota(jnp.int32, (1, LANES), 1)
        weighted = area[pl.ds(block, 1), :] * (block * LANES + lanes < live[0]).astype(F32)

        def store(m, v, step, value):
            ssend[c, m // 2, m % 2, v : v + step, :] = value

        row = score_block(frecv.at[c], y_block, weighted, store)
        srecv[c, e] = ssend[c, e]
        return row

    def scored_send(c):
        return spread(
            "x", lambda k: ssend.at[c, k], lambda d, own: srecv.at[c, own], s_rs.at[c], srecv.at[c, pl.ds(0, 3)]
        )

    def backward(c, lo, wide):
        s, cols = pl.ds(c * CHUNK, CHUNK), slice(lo, lo + wide)
        for m in range(2):
            slopes = jnp.concatenate([srecv[c, k, m] for k in range(4)], axis=1)
            bh = dot(slopes, wout[:, cols], 0, 0)
            back[m, s, cols] = (back[m, s, cols].astype(F32) * bh).astype(BF16)

    def output_part(c):
        s = pl.ds(c * CHUNK, CHUNK)
        slopes = jnp.concatenate([srecv[c, k, m] for m in range(2) for k in range(4)], axis=1)
        term = dot(slopes, hid[:, s, :].reshape(2 * CHUNK, FEATURES), 1, 0)
        if c == 0:
            gout[...] = term
        else:
            gout[...] += term

    def weight_early():
        a = lat[:, :CHUNK, :].reshape(2 * CHUNK, FEATURES)
        term = dot(a, back[:, :CHUNK, :].reshape(2 * CHUNK, FEATURES), 0, 0)
        for i in range(2):
            acc[i] = term[:, i * HALF : (i + 1) * HALF].reshape(16, 2, ROWS, HALF)

    def weight_half(i):
        cols = slice(i * HALF, (i + 1) * HALF)
        a = lat[:, CHUNK:, :].reshape(2 * CHUNK, FEATURES)
        acc[i] += dot(a, back[:, CHUNK:, cols].reshape(2 * CHUNK, HALF), 0, 0).reshape(16, 2, ROWS, HALF)

    def g_start():
        def body(k, _):
            cols = pl.ds(pl.multiple_of((k * 2 + 1 - core) * LANES, LANES), LANES)
            g_core_send[k] = gout[:, cols].astype(BF16)
            return 0

        lax.fori_loop(0, 4, body, 0)
        return send([(g_core_send, g_core_recv, sibling)], g_rs.at[0], g_core_recv)

    def g_to_first(arrived):
        arrived()

        def body(k, _):
            cols = pl.ds(pl.multiple_of((k * 2 + core) * LANES, LANES), LANES)
            g_one_send[k] = (gout[:, cols] + g_core_recv[k].astype(F32)).astype(BF16)
            return 0

        lax.fori_loop(0, 4, body, 0)
        return spread("y", lambda k: g_one_send.at[k], lambda d, own: g_one_recv.at[d - 1], g_rs.at[1], g_one_recv)

    def g_to_second(arrived):
        arrived()
        g_two[e] = received(g_one_send[y], g_one_recv).astype(BF16)
        return share("x", g_two, g_rs.at[2])

    def g_to_third(arrived):
        arrived()
        g_three[z] = four(g_two).astype(BF16)
        return share("z", g_three, g_rs.at[3])

    def g_to_all(arrived, share_of):
        arrived()
        g_all[core, y] = (four(g_three) * share_of).astype(BF16)
        return spread("y", lambda k: g_all.at[core, y], lambda d, own: g_all.at[core, own], g_rs.at[4], g_all.at[0, pl.ds(0, 3)])

    def g_to_sibling(arrived):
        arrived()
        return send([(g_all.at[core], g_all.at[core], sibling)], g_rs.at[5], g_all.at[0])

    def g_finish(arrived):
        arrived()
        for k in range(8):
            gwout_out[:, k * LANES : (k + 1) * LANES] = g_all[k % 2, k // 2].astype(F32)

    def to_core(i):
        core_send[i] = acc[i, :, 1 - core].astype(BF16)
        return send([(core_send.at[i], core_recv.at[i], sibling)], p_rs.at[i], core_recv.at[i])

    def from_core(i, lo, wide):
        cols = slice(lo, lo + wide)
        return (acc[i, :, core, :, cols] + core_recv[i, :, :, cols].astype(F32)).astype(BF16)

    def part(j, k):
        return one_send[j].at[k] if PIECES[j][3] == "y" else one_send[j].at[:, k]

    def to_first(j):
        half, lo, wide, axis = PIECES[j]
        one_send[j][...] = from_core(half, lo, wide).reshape(4, 4, ROWS, wide)
        return spread(
            axis, lambda k: part(j, k), lambda d, own: one_recv[j].at[d - 1], p_rs.at[2 + j], one_recv[j]
        )

    def to_second(j, arrived):
        arrived()
        axis = PIECES[j][3]
        two_send[j][...] = received(part(j, place[axis])[...], one_recv[j]).astype(BF16)
        return spread(
            "z" if axis == "y" else "y", lambda k: two_send[j].at[k], lambda d, own: two_recv[j].at[d - 1],
            p_rs.at[6 + j], two_recv[j],
        )

    def to_third(i, arrived):
        for j in (2 * i, 2 * i + 1):
            arrived[j]()
            wide, own = PIECES[j][2], place["z" if PIECES[j][3] == "y" else "y"]
            lo = (j % 2) * wide
            three[i][e, :, lo : lo + wide] = received(two_send[j][own], two_recv[j]).astype(BF16)
        return share("x", three[i], p_rs.at[10 + i])

    def finish(i, arrived, share_of):
        arrived()
        wide = 2 * PIECES[2 * i][2]
        gwin_out[:, FEATURES // 4 * (1 + i) : FEATURES // 4 * (1 + i) + wide] = four(three[i]) * share_of

    def x_block(k):
        return slice((k // 2) * 16, (k // 2 + 1) * 16), slice((k % 2) * LANES, (k % 2 + 1) * LANES)

    def x_first():
        total = from_core(0, 0, 2 * LANES)
        for k in range(4):
            rows, cols = x_block(k)
            x_send[k] = total[:, rows, cols]
        return spread("x", lambda k: x_send.at[k], lambda d, own: x_recv.at[d - 1], p_rs.at[12], x_recv)

    def x_second(arrived):
        arrived()
        xy_send[...] = received(x_send[e], x_recv).astype(BF16).reshape(4, 4, 16, LANES)
        return spread("y", lambda k: xy_send.at[k], lambda d, own: xy_recv.at[d - 1], p_rs.at[13], xy_recv)

    def x_third(arrived):
        arrived()
        xz_send[...] = received(xy_send[y], xy_recv).astype(BF16)
        slot = e * 4 + z
        x_all[slot] = xz_send[z]
        copies = []
        for dx, dz in sorted(((i, j) for i in range(4) for j in range(4) if i or j), key=lambda h: h not in FAR):
            to = turn(z, dz)
            copies.append((xz_send.at[to], x_all.at[slot], device(turn(e, dx), y, to, core)))
        return send(copies, p_rs.at[14], x_all.at[pl.ds(0, 15)])

    def x_finish(arrived, share_of):
        arrived()
        for k in range(4):
            rows, cols = x_block(k)
            gwin_out[rows, cols] = four(x_all.at[pl.ds(4 * k, 4)]) * share_of

    def latent_tile(i, factor):
        m, s = i // 2, pl.ds((i % 2) * CHUNK, CHUNK)
        glat_out[m, s, :] = (dot(back[m, s, :], w[...], 1, 1) * factor).astype(BF16)

    def block(run, *args):
        pl.when(core < 2)(lambda: run(*args))

    loads[0, 0].wait()
    load_w[0].wait()
    loads[0, 1].start()
    for i in range(2):
        cols = slice(i * HALF, (i + 1) * HALF)
        if i == 1:
            load_w[1].wait()
            loads[1, 0].start()
            loads[1, 1].start()
        block(forward_first, cols)
    small[1].wait()
    block(forecast, 0, 0)
    pl.semaphore_wait(barrier, len(peers))
    f00 = forward_send(0, 0)
    loads[0, 1].wait()
    block(forward, 0, 1)
    f01 = forward_send(0, 1)
    loads[1, 0].wait()
    block(forward, 1, 0)
    f10 = forward_send(1, 0)
    loads[1, 1].wait()
    block(forward_half, 1, 1, (2, 1))
    f11 = forward_send(1, 1, (2, 1))
    f00()
    f01()
    small[0].wait()
    small[2].wait()
    row0 = scored(0)
    s0 = scored_send(0)
    block(forward_half, 1, 1, (3, 0))
    forward_send(1, 1, (3,))
    frecv[1, e, 1] = fsend[1, e, 1]
    block(slopes_of_gelu, 0, 1)
    block(slopes_of_gelu, 1, 0)
    block(slopes_of_gelu, 1, 1)
    f10()
    f11()
    row1 = scored(1)
    s1 = scored_send(1)
    ls_core[core] = sums_tile(row0 + row1)
    lc = send([(ls_core.at[core], ls_core.at[core], sibling)], t_rs.at[0], ls_core.at[0])
    s0()
    block(backward, 0, 0, FEATURES)
    block(output_part, 0)
    lc()
    ls_y[y] = ls_core[0] + ls_core[1]
    lc = share("y", ls_y, t_rs.at[1])
    block(weight_early)
    s1()
    block(output_part, 1)
    g = g_start()
    lc()
    ls_z[z] = four(ls_y)
    lc = share("z", ls_z, t_rs.at[2])
    block(backward, 1, 0, HALF)
    block(weight_half, 0)
    c0 = to_core(0)
    g = g_to_first(g)
    block(backward, 1, HALF, HALF)
    block(weight_half, 1)
    c1 = to_core(1)
    c0()
    p = {}
    xf = x_first()
    p[0] = to_first(0)
    p[1] = to_first(1)
    lc()
    sums = four(ls_z)
    ls_x[e] = sums
    lc = share("x", ls_x, t_rs.at[3])
    totals = jnp.sum(sums, axis=1, keepdims=True)
    weight_total, live_total = totals[1:2, 0:1], totals[2:3, 0:1]
    factor = LOSS_SCALE * live_total / weight_total
    block(latent_tile, 0, factor)
    g = g_to_second(g)
    c1()
    p[2] = to_first(2)
    p[3] = to_first(3)
    block(latent_tile, 1, factor)
    block(latent_tile, 2, factor)
    xf = x_second(xf)
    p[0] = to_second(0, p[0])
    p[1] = to_second(1, p[1])
    g = g_to_third(g)
    block(latent_tile, 3, factor)
    lc()
    loss_out[...] = jnp.sum(four(ls_x), axis=1, keepdims=True) / weight_total + jnp.zeros((8, LANES), F32)
    share_of = LOSS_SCALE / weight_total
    p[2] = to_second(2, p[2])
    p[3] = to_second(3, p[3])
    xf = x_third(xf)
    xa = to_third(0, p)
    g = g_to_all(g, share_of)
    xb = to_third(1, p)
    finish(0, xa, share_of)
    g = g_to_sibling(g)
    x_finish(xf, share_of)
    g_finish(g)
    finish(1, xb, share_of)
    for left in leaving.values():
        left()


def write_out(loss, glat, gwin, gwout, loss_out, glat_out, gwin_out, gwout_out, sem):
    pairs = [(glat, glat_out), (gwin, gwin_out), (gwout, gwout_out)]
    cps = [pltpu.make_async_copy(src, dst, sem.at[i]) for i, (src, dst) in enumerate(pairs)]
    for cp in cps:
        cp.start()
    loss_out[...] = loss[0:1, 0:1]
    for cp in cps:
        cp.wait()


def per_device(latent, w_in, output_weight, targets, area_weights, live_counts):
    vmem = pl.BlockSpec(memory_space=pltpu.VMEM)
    hbm = pl.BlockSpec(memory_space=pl.ANY)
    V = pltpu.VMEM
    dma = pltpu.SemaphoreType.DMA
    widths = [p[2] for p in PIECES]
    scratch = [
        V((2, POINTS, FEATURES), BF16),
        V((2, POINTS, FEATURES), F32),
        V((FEATURES, FEATURES), BF16),
        V((VARS, FEATURES), BF16),
        V((VARS, POINTS), BF16),
        V((8, LANES), F32),
        V((2, POINTS, FEATURES), BF16),
        V((2, POINTS, FEATURES), BF16),
        V((2, 16, 2, ROWS, HALF), F32),
        V((CHUNKS, 4, 2, VARS, LANES), BF16),
        V((CHUNKS, 4, 2, VARS, LANES), BF16),
        V((CHUNKS, 4, 2, VARS, LANES), BF16),
        V((CHUNKS, 4, 2, VARS, LANES), BF16),
        V((VARS, FEATURES), F32),
        V((2, 16, ROWS, HALF), BF16),
        V((2, 16, ROWS, HALF), BF16),
        [V((4, 4, ROWS, n), BF16) for n in widths],
        [V((3, 4, ROWS, n), BF16) for n in widths],
        [V((4, ROWS, n), BF16) for n in widths],
        [V((3, ROWS, n), BF16) for n in widths],
        [V((4, ROWS, 2 * widths[0]), BF16), V((4, ROWS, 2 * widths[2]), BF16)],
        V((4, 16, 16, LANES), BF16),
        V((3, 16, 16, LANES), BF16),
        V((4, 4, 16, LANES), BF16),
        V((3, 4, 16, LANES), BF16),
        V((4, 16, LANES), BF16),
        V((16, 16, LANES), BF16),
        V((4, VARS, LANES), BF16),
        V((4, VARS, LANES), BF16),
        V((4, VARS, LANES), BF16),
        V((3, VARS, LANES), BF16),
        V((4, VARS, LANES), BF16),
        V((4, VARS, LANES), BF16),
        V((2, 4, VARS, LANES), BF16),
        V((2, 8, LANES), F32),
        V((4, 8, LANES), F32),
        V((4, 8, LANES), F32),
        V((4, 8, LANES), F32),
        dma((11,)),
        dma((SENDS,)),
        dma((CHUNKS, 2)),
        dma((CHUNKS,)),
        dma((15,)),
        dma((6,)),
        dma((4,)),
    ]
    operands = (latent, w_in, output_weight, targets, area_weights.reshape(8, LANES))
    results = pl.pallas_call(
        kernel,
        out_shape=[
            V((8, LANES), F32),
            V(latent.shape, BF16),
            V((ROWS, FEATURES), F32),
            V((VARS, FEATURES), F32),
        ],
        in_specs=[pl.BlockSpec(memory_space=pltpu.HBM)] * 5 + [pl.BlockSpec(memory_space=pltpu.SMEM)],
        out_specs=[vmem] * 4,
        scratch_shapes=scratch,
        compiler_params=pltpu.CompilerParams(collective_id=1, has_side_effects=True, vmem_limit_bytes=48 << 20),
        name="energy_step",
    )(*[pltpu.with_memory_space_constraint(a, pltpu.HBM) for a in operands], live_counts)
    loss, glat, gwin, gwout = pl.pallas_call(
        write_out,
        out_shape=[
            jax.ShapeDtypeStruct((1, 1), F32),
            jax.ShapeDtypeStruct(latent.shape, BF16),
            jax.ShapeDtypeStruct((ROWS, FEATURES), F32),
            jax.ShapeDtypeStruct((VARS, FEATURES), F32),
        ],
        in_specs=[vmem] * 4,
        out_specs=[vmem] + [hbm] * 3,
        scratch_shapes=[dma((3,))],
        compiler_params=pltpu.CompilerParams(vmem_limit_bytes=1 << 20),
        name="write_out",
    )(*[pltpu.with_memory_space_constraint(r, pltpu.VMEM) for r in results])
    return loss.reshape(()), glat, gwin, gwout


def solution(mesh):
    placed = (P("ens", "sp", None), P(), P(), P(None, "sp"), P("sp"), P("sp"))
    return jax.shard_map(
        per_device,
        mesh=mesh,
        in_specs=placed,
        out_specs=(P(), P("ens", "sp", None), P("sp", None), P()),
        check_vma=False,
    )
```

```python
import functools
import math

import jax
import jax.numpy as jnp
from jax import lax
from jax.experimental import pallas as pl
from jax.experimental.pallas import tpu as pltpu
from jax.sharding import PartitionSpec as P

BF16, F32 = jnp.bfloat16, jnp.float32
MESH = pl.DeviceIdType.MESH
LOSS_SCALE = 1024.0
MEMBERS, VARS, FEATURES, POINTS = 8, 80, 1024, 1024
CHUNKS = 2
CHUNK = POINTS // CHUNKS
LANES = 128
HALF = FEATURES // 2
PIECES = ((0, 256, 128, "y"), (0, 384, 128, "z"), (1, 0, 256, "y"), (1, 256, 256, "z"))
SENDS = 8
FAR = ((2, 2), (2, 1), (2, 3), (1, 2), (3, 2))
ROWS = 32
OUTER = math.sqrt(2.0 / math.pi)
INNER = OUTER * 0.044715


def dot(a, b, ca, cb):
    return lax.dot_general(a, b, (((ca,), (cb,)), ((), ())), preferred_element_type=F32)


def activation(z):
    cubic = INNER * (z * z)
    s = 0.5 * jnp.tanh(z * (cubic + OUTER)) + 0.5
    h = z * s
    slope = s + (h - h * s) * (6.0 * cubic + 2.0 * OUTER)
    return h.astype(BF16), slope.astype(BF16)


def activation_only(z):
    return (z * (0.5 * jnp.tanh(z * (INNER * (z * z) + OUTER)) + 0.5)).astype(BF16)


def score_block(x_ref, y, weighted, store):
    n = MEMBERS
    pairs = [(i, j) for i in range(n) for j in range(i + 1, n)]
    step = 16
    own = [jnp.zeros((step, LANES), F32) for _ in range(n)]
    between = [jnp.zeros((step, LANES), F32) for _ in pairs]
    for v in range(0, VARS, step):
        x = [x_ref[m // 2, m % 2, v : v + step, :].astype(F32) for m in range(n)]
        for m in range(n):
            d = x[m] - y[v : v + step]
            own[m] = own[m] + d * d
        for q, (i, j) in enumerate(pairs):
            d = x[i] - x[j]
            between[q] = between[q] + d * d
    a = [jnp.sqrt(jnp.sum(o, axis=0, keepdims=True) + 1.0) for o in own]
    b = [jnp.sqrt(jnp.sum(o, axis=0, keepdims=True) + 1.0) for o in between]
    score = sum(a) / n - sum(b) / (n * (n - 1.0))
    from_target = [weighted / (n * t) for t in a]
    from_pair = [weighted / (n * (n - 1.0) * t) for t in b]
    for v in range(0, VARS, step):
        x = [x_ref[m // 2, m % 2, v : v + step, :].astype(F32) for m in range(n)]
        total = [(x[m] - y[v : v + step]) * from_target[m] for m in range(n)]
        for q, (i, j) in enumerate(pairs):
            d = (x[i] - x[j]) * from_pair[q]
            total[i] = total[i] - d
            total[j] = total[j] + d
        for m in range(n):
            store(m, v, step, total[m].astype(BF16))
    return weighted * score


def kernel(
    lat_hbm, w_hbm, wout_hbm, targets_hbm, area_hbm, live,
    loss_out, glat_out, gwin_out, gwout_out,
    lat, later, w, wout, targets, area, hid, back, acc, fsend, frecv, ssend, srecv, gout,
    core_send, core_recv, one_send, one_recv, two_send, two_recv, three,
    x_send, x_recv, xy_send, xy_recv, xz_send, x_all,
    g_core_send, g_core_recv, g_one_send, g_one_recv, g_two, g_three, g_all,
    ls_core, ls_y, ls_z, ls_x,
    in_sem, out_sem, f_rs, s_rs, p_rs, g_rs, t_rs,
):
    e = lax.axis_index("ens")
    sp = lax.axis_index("sp")
    core = lax.rem(sp, 2)
    z = lax.rem(sp // 2, 4)
    y = sp // 8

    def turn(i, d):
        return lax.rem(i + d, 4)

    def device(x_, y_, z_, core_):
        return (x_, (y_ * 4 + z_) * 2 + core_)

    along = {
        "x": lambda d: device(turn(e, d), y, z, core),
        "y": lambda d: device(e, turn(y, d), z, core),
        "z": lambda d: device(e, y, turn(z, d), core),
    }
    place = {"x": e, "y": y, "z": z}
    sibling = device(e, y, z, 1 - core)

    def load(m, c):
        s = pl.ds(c * CHUNK, CHUNK)
        return pltpu.make_async_copy(lat_hbm.at[m, s], lat.at[m, s], in_sem.at[2 * c + m])

    loads = {(c, m): load(m, c) for c in range(CHUNKS) for m in range(2)}
    small = [
        pltpu.make_async_copy(src, dst, in_sem.at[8 + i])
        for i, (src, dst) in enumerate([(area_hbm, area), (wout_hbm, wout), (targets_hbm, targets)])
    ]
    loads[0, 0].start()
    load_w = []
    for i in range(2):
        cols = pl.ds(i * HALF, HALF)
        load_w.append(pltpu.make_async_copy(w_hbm.at[:, cols], w.at[:, cols], in_sem.at[4 + i]))
        load_w[i].start()
    for cp in small:
        cp.start()

    peers = [along[k](d) for k in "xyz" for d in (1, 2, 3)] + [sibling]
    peers += [device(turn(e, dx), y, turn(z, dz), core) for dx in (1, 2, 3) for dz in (1, 2, 3)]
    barrier = pltpu.get_barrier_semaphore()
    for p in peers:
        pl.semaphore_signal(barrier, inc=1, device_id=p, device_id_type=MESH)

    def remote(src, dst, ss, rs, to):
        return pltpu.make_async_remote_copy(
            src_ref=src, dst_ref=dst, send_sem=ss, recv_sem=rs, device_id=to, device_id_type=MESH
        )

    leaving = {}
    turns = [0]

    def send(copies, rs, whole, sent=None):
        k = turns[0] % SENDS
        turns[0] += 1
        if k in leaving:
            leaving.pop(k)()
        ss = out_sem.at[k]
        for src, dst, to in copies:
            remote(src, dst, ss, rs, to).start()
        sent = whole if sent is None else sent
        leaving[k] = lambda: remote(sent, sent, ss, rs, sibling).wait_send()
        return lambda: remote(whole, whole, ss, rs, sibling).wait_recv()

    def spread(axis, src, dst, rs, whole, sent=None, hops=(2, 1, 3)):
        own = place[axis]
        return send([(src(turn(own, d)), dst(d, own), along[axis](d)) for d in hops], rs, whole, sent)

    def share(axis, buf, rs):
        return spread(axis, lambda k: buf.at[place[axis]], lambda d, own: buf.at[own], rs, buf.at[pl.ds(0, 3)])

    def four(ref):
        return (ref[0].astype(F32) + ref[1].astype(F32)) + (ref[2].astype(F32) + ref[3].astype(F32))

    def received(own, ref):
        total = own.astype(F32)
        for d in range(3):
            total = total + ref[d].astype(F32)
        return total

    def sums_tile(scores):
        where = lax.broadcasted_iota(jnp.int32, (8, LANES), 0) * LANES + lax.broadcasted_iota(jnp.int32, (8, LANES), 1)
        is_live = (where < live[0]).astype(F32)
        row = lax.broadcasted_iota(jnp.int32, (8, LANES), 0)
        weights = jnp.sum(area[...] * is_live, axis=0, keepdims=True)
        return jnp.where(row == 0, scores, jnp.where(row == 1, weights, jnp.sum(is_live, axis=0, keepdims=True)))

    def slopes_of_gelu(c, m):
        s = pl.ds(c * CHUNK, CHUNK)
        back[m, s, :] = activation(later[m, s, :])[1]

    def forecast(c, m):
        f = dot(wout[...], hid[m, c * CHUNK : (c + 1) * CHUNK, :], 1, 1).astype(BF16)
        for k in range(4):
            fsend[c, k, m] = f[:, k * LANES : (k + 1) * LANES]
        frecv[c, e, m] = fsend[c, e, m]

    def forward(c, m):
        s = pl.ds(c * CHUNK, CHUNK)
        pre = jnp.dot(lat[m, s, :], w[...], preferred_element_type=F32)
        hid[m, s, :] = activation_only(pre)
        later[m, s, :] = pre
        forecast(c, m)

    def forward_first(cols):
        pre = jnp.dot(lat[0, :CHUNK, :], w[:, cols], preferred_element_type=F32)
        hid[0, :CHUNK, cols], back[0, :CHUNK, cols] = activation(pre)

    def forward_send(c, m, hops=(2, 1, 3)):
        return spread(
            "x", lambda k: fsend.at[c, k, m], lambda d, own: frecv.at[c, own, m], f_rs.at[c, m],
            frecv.at[c, pl.ds(0, 3), m], frecv.at[c, pl.ds(0, len(hops)), m], hops,
        )

    def forward_half(c, m, hops):
        rows = [pl.ds(pl.multiple_of(c * CHUNK + turn(e, d) * LANES, LANES), LANES) for d in hops]
        pre = jnp.dot(
            jnp.concatenate([lat[m, r, :] for r in rows], axis=0), w[...], preferred_element_type=F32
        )
        h = activation_only(pre)
        for i, r in enumerate(rows):
            hid[m, r, :] = h[i * LANES : (i + 1) * LANES]
            later[m, r, :] = pre[i * LANES : (i + 1) * LANES]
        f = dot(wout[...], h, 1, 1).astype(BF16)
        for i, d in enumerate(hops):
            fsend[c, turn(e, d), m] = f[:, i * LANES : (i + 1) * LANES]

    def scored(c):
        block = c * 4 + e
        y_block = targets[:, pl.ds(pl.multiple_of(block * LANES, LANES), LANES)].astype(F32)
        lanes = lax.broadcasted_iota(jnp.int32, (1, LANES), 1)
        weighted = area[pl.ds(block, 1), :] * (block * LANES + lanes < live[0]).astype(F32)

        def store(m, v, step, value):
            ssend[c, m // 2, m % 2, v : v + step, :] = value

        row = score_block(frecv.at[c], y_block, weighted, store)
        srecv[c, e] = ssend[c, e]
        return row

    def scored_send(c):
        return spread(
            "x", lambda k: ssend.at[c, k], lambda d, own: srecv.at[c, own], s_rs.at[c], srecv.at[c, pl.ds(0, 3)]
        )

    def backward(c, lo, wide):
        s, cols = pl.ds(c * CHUNK, CHUNK), slice(lo, lo + wide)
        for m in range(2):
            slopes = jnp.concatenate([srecv[c, k, m] for k in range(4)], axis=1)
            bh = dot(slopes, wout[:, cols], 0, 0)
            back[m, s, cols] = (back[m, s, cols].astype(F32) * bh).astype(BF16)

    def output_part(c):
        s = pl.ds(c * CHUNK, CHUNK)
        slopes = jnp.concatenate([srecv[c, k, m] for m in range(2) for k in range(4)], axis=1)
        term = dot(slopes, hid[:, s, :].reshape(2 * CHUNK, FEATURES), 1, 0)
        if c == 0:
            gout[...] = term
        else:
            gout[...] += term

    def weight_early():
        a = lat[:, :CHUNK, :].reshape(2 * CHUNK, FEATURES)
        term = dot(a, back[:, :CHUNK, :].reshape(2 * CHUNK, FEATURES), 0, 0)
        for i in range(2):
            acc[i] = term[:, i * HALF : (i + 1) * HALF].reshape(16, 2, ROWS, HALF)

    def weight_half(i):
        cols = slice(i * HALF, (i + 1) * HALF)
        a = lat[:, CHUNK:, :].reshape(2 * CHUNK, FEATURES)
        acc[i] += dot(a, back[:, CHUNK:, cols].reshape(2 * CHUNK, HALF), 0, 0).reshape(16, 2, ROWS, HALF)

    def g_start():
        def body(k, _):
            cols = pl.ds(pl.multiple_of((k * 2 + 1 - core) * LANES, LANES), LANES)
            g_core_send[k] = gout[:, cols].astype(BF16)
            return 0

        lax.fori_loop(0, 4, body, 0)
        return send([(g_core_send, g_core_recv, sibling)], g_rs.at[0], g_core_recv)

    def g_to_first(arrived):
        arrived()

        def body(k, _):
            cols = pl.ds(pl.multiple_of((k * 2 + core) * LANES, LANES), LANES)
            g_one_send[k] = (gout[:, cols] + g_core_recv[k].astype(F32)).astype(BF16)
            return 0

        lax.fori_loop(0, 4, body, 0)
        return spread("y", lambda k: g_one_send.at[k], lambda d, own: g_one_recv.at[d - 1], g_rs.at[1], g_one_recv)

    def g_to_second(arrived):
        arrived()
        g_two[e] = received(g_one_send[y], g_one_recv).astype(BF16)
        return share("x", g_two, g_rs.at[2])

    def g_to_third(arrived):
        arrived()
        g_three[z] = four(g_two).astype(BF16)
        return share("z", g_three, g_rs.at[3])

    def g_to_all(arrived, share_of):
        arrived()
        g_all[core, y] = (four(g_three) * share_of).astype(BF16)
        return spread("y", lambda k: g_all.at[core, y], lambda d, own: g_all.at[core, own], g_rs.at[4], g_all.at[0, pl.ds(0, 3)])

    def g_to_sibling(arrived):
        arrived()
        return send([(g_all.at[core], g_all.at[core], sibling)], g_rs.at[5], g_all.at[0])

    def g_finish(arrived):
        arrived()
        for k in range(8):
            gwout_out[:, k * LANES : (k + 1) * LANES] = g_all[k % 2, k // 2].astype(F32)

    def to_core(i):
        core_send[i] = acc[i, :, 1 - core].astype(BF16)
        return send([(core_send.at[i], core_recv.at[i], sibling)], p_rs.at[i], core_recv.at[i])

    def from_core(i, lo, wide):
        cols = slice(lo, lo + wide)
        return (acc[i, :, core, :, cols] + core_recv[i, :, :, cols].astype(F32)).astype(BF16)

    def part(j, k):
        return one_send[j].at[k] if PIECES[j][3] == "y" else one_send[j].at[:, k]

    def to_first(j):
        half, lo, wide, axis = PIECES[j]
        one_send[j][...] = from_core(half, lo, wide).reshape(4, 4, ROWS, wide)
        return spread(
            axis, lambda k: part(j, k), lambda d, own: one_recv[j].at[d - 1], p_rs.at[2 + j], one_recv[j]
        )

    def to_second(j, arrived):
        arrived()
        axis = PIECES[j][3]
        two_send[j][...] = received(part(j, place[axis])[...], one_recv[j]).astype(BF16)
        return spread(
            "z" if axis == "y" else "y", lambda k: two_send[j].at[k], lambda d, own: two_recv[j].at[d - 1],
            p_rs.at[6 + j], two_recv[j],
        )

    def to_third(i, arrived):
        for j in (2 * i, 2 * i + 1):
            arrived[j]()
            wide, own = PIECES[j][2], place["z" if PIECES[j][3] == "y" else "y"]
            lo = (j % 2) * wide
            three[i][e, :, lo : lo + wide] = received(two_send[j][own], two_recv[j]).astype(BF16)
        return share("x", three[i], p_rs.at[10 + i])

    def finish(i, arrived, share_of):
        arrived()
        wide = 2 * PIECES[2 * i][2]
        gwin_out[:, FEATURES // 4 * (1 + i) : FEATURES // 4 * (1 + i) + wide] = four(three[i]) * share_of

    def x_block(k):
        return slice((k // 2) * 16, (k // 2 + 1) * 16), slice((k % 2) * LANES, (k % 2 + 1) * LANES)

    def x_first():
        total = from_core(0, 0, 2 * LANES)
        for k in range(4):
            rows, cols = x_block(k)
            x_send[k] = total[:, rows, cols]
        return spread("x", lambda k: x_send.at[k], lambda d, own: x_recv.at[d - 1], p_rs.at[12], x_recv)

    def x_second(arrived):
        arrived()
        xy_send[...] = received(x_send[e], x_recv).astype(BF16).reshape(4, 4, 16, LANES)
        return spread("y", lambda k: xy_send.at[k], lambda d, own: xy_recv.at[d - 1], p_rs.at[13], xy_recv)

    def x_third(arrived):
        arrived()
        xz_send[...] = received(xy_send[y], xy_recv).astype(BF16)
        slot = e * 4 + z
        x_all[slot] = xz_send[z]
        copies = []
        for dx, dz in sorted(((i, j) for i in range(4) for j in range(4) if i or j), key=lambda h: h not in FAR):
            to = turn(z, dz)
            copies.append((xz_send.at[to], x_all.at[slot], device(turn(e, dx), y, to, core)))
        return send(copies, p_rs.at[14], x_all.at[pl.ds(0, 15)])

    def x_finish(arrived, share_of):
        arrived()
        for k in range(4):
            rows, cols = x_block(k)
            gwin_out[rows, cols] = four(x_all.at[pl.ds(4 * k, 4)]) * share_of

    def latent_tile(i, factor):
        m, s = i // 2, pl.ds((i % 2) * CHUNK, CHUNK)
        glat_out[m, s, :] = (dot(back[m, s, :], w[...], 1, 1) * factor).astype(BF16)

    def block(run, *args):
        pl.when(core < 2)(lambda: run(*args))

    loads[0, 0].wait()
    load_w[0].wait()
    loads[0, 1].start()
    for i in range(2):
        cols = slice(i * HALF, (i + 1) * HALF)
        if i == 1:
            load_w[1].wait()
            loads[1, 0].start()
            loads[1, 1].start()
        block(forward_first, cols)
    small[1].wait()
    block(forecast, 0, 0)
    pl.semaphore_wait(barrier, len(peers))
    f00 = forward_send(0, 0)
    loads[0, 1].wait()
    block(forward, 0, 1)
    f01 = forward_send(0, 1)
    loads[1, 0].wait()
    block(forward, 1, 0)
    f10 = forward_send(1, 0)
    loads[1, 1].wait()
    block(forward_half, 1, 1, (2, 1))
    f11 = forward_send(1, 1, (2, 1))
    f00()
    f01()
    small[0].wait()
    small[2].wait()
    row0 = scored(0)
    s0 = scored_send(0)
    block(forward_half, 1, 1, (3, 0))
    forward_send(1, 1, (3,))
    frecv[1, e, 1] = fsend[1, e, 1]
    block(slopes_of_gelu, 0, 1)
    block(slopes_of_gelu, 1, 0)
    block(slopes_of_gelu, 1, 1)
    f10()
    f11()
    row1 = scored(1)
    s1 = scored_send(1)
    ls_core[core] = sums_tile(row0 + row1)
    lc = send([(ls_core.at[core], ls_core.at[core], sibling)], t_rs.at[0], ls_core.at[0])
    s0()
    block(backward, 0, 0, FEATURES)
    block(output_part, 0)
    lc()
    ls_y[y] = ls_core[0] + ls_core[1]
    lc = share("y", ls_y, t_rs.at[1])
    block(weight_early)
    s1()
    block(output_part, 1)
    g = g_start()
    lc()
    ls_z[z] = four(ls_y)
    lc = share("z", ls_z, t_rs.at[2])
    block(backward, 1, 0, HALF)
    block(weight_half, 0)
    c0 = to_core(0)
    g = g_to_first(g)
    block(backward, 1, HALF, HALF)
    block(weight_half, 1)
    c1 = to_core(1)
    c0()
    p = {}
    xf = x_first()
    p[0] = to_first(0)
    p[1] = to_first(1)
    lc()
    sums = four(ls_z)
    ls_x[e] = sums
    lc = share("x", ls_x, t_rs.at[3])
    totals = jnp.sum(sums, axis=1, keepdims=True)
    weight_total, live_total = totals[1:2, 0:1], totals[2:3, 0:1]
    factor = LOSS_SCALE * live_total / weight_total
    c1()
    p[2] = to_first(2)
    p[3] = to_first(3)
    block(latent_tile, 0, factor)
    g = g_to_second(g)
    block(latent_tile, 1, factor)
    block(latent_tile, 2, factor)
    xf = x_second(xf)
    p[0] = to_second(0, p[0])
    p[1] = to_second(1, p[1])
    g = g_to_third(g)
    block(latent_tile, 3, factor)
    lc()
    loss_out[...] = jnp.sum(four(ls_x), axis=1, keepdims=True) / weight_total + jnp.zeros((8, LANES), F32)
    share_of = LOSS_SCALE / weight_total
    p[2] = to_second(2, p[2])
    p[3] = to_second(3, p[3])
    xf = x_third(xf)
    xa = to_third(0, p)
    g = g_to_all(g, share_of)
    xb = to_third(1, p)
    finish(0, xa, share_of)
    g = g_to_sibling(g)
    x_finish(xf, share_of)
    g_finish(g)
    finish(1, xb, share_of)
    for left in leaving.values():
        left()


def write_out(loss, glat, gwin, gwout, loss_out, glat_out, gwin_out, gwout_out, sem):
    pairs = [(glat, glat_out), (gwin, gwin_out), (gwout, gwout_out)]
    cps = [pltpu.make_async_copy(src, dst, sem.at[i]) for i, (src, dst) in enumerate(pairs)]
    for cp in cps:
        cp.start()
    loss_out[...] = loss[0:1, 0:1]
    for cp in cps:
        cp.wait()


def per_device(latent, w_in, output_weight, targets, area_weights, live_counts):
    vmem = pl.BlockSpec(memory_space=pltpu.VMEM)
    hbm = pl.BlockSpec(memory_space=pl.ANY)
    V = pltpu.VMEM
    dma = pltpu.SemaphoreType.DMA
    widths = [p[2] for p in PIECES]
    scratch = [
        V((2, POINTS, FEATURES), BF16),
        V((2, POINTS, FEATURES), F32),
        V((FEATURES, FEATURES), BF16),
        V((VARS, FEATURES), BF16),
        V((VARS, POINTS), BF16),
        V((8, LANES), F32),
        V((2, POINTS, FEATURES), BF16),
        V((2, POINTS, FEATURES), BF16),
        V((2, 16, 2, ROWS, HALF), F32),
        V((CHUNKS, 4, 2, VARS, LANES), BF16),
        V((CHUNKS, 4, 2, VARS, LANES), BF16),
        V((CHUNKS, 4, 2, VARS, LANES), BF16),
        V((CHUNKS, 4, 2, VARS, LANES), BF16),
        V((VARS, FEATURES), F32),
        V((2, 16, ROWS, HALF), BF16),
        V((2, 16, ROWS, HALF), BF16),
        [V((4, 4, ROWS, n), BF16) for n in widths],
        [V((3, 4, ROWS, n), BF16) for n in widths],
        [V((4, ROWS, n), BF16) for n in widths],
        [V((3, ROWS, n), BF16) for n in widths],
        [V((4, ROWS, 2 * widths[0]), BF16), V((4, ROWS, 2 * widths[2]), BF16)],
        V((4, 16, 16, LANES), BF16),
        V((3, 16, 16, LANES), BF16),
        V((4, 4, 16, LANES), BF16),
        V((3, 4, 16, LANES), BF16),
        V((4, 16, LANES), BF16),
        V((16, 16, LANES), BF16),
        V((4, VARS, LANES), BF16),
        V((4, VARS, LANES), BF16),
        V((4, VARS, LANES), BF16),
        V((3, VARS, LANES), BF16),
        V((4, VARS, LANES), BF16),
        V((4, VARS, LANES), BF16),
        V((2, 4, VARS, LANES), BF16),
        V((2, 8, LANES), F32),
        V((4, 8, LANES), F32),
        V((4, 8, LANES), F32),
        V((4, 8, LANES), F32),
        dma((11,)),
        dma((SENDS,)),
        dma((CHUNKS, 2)),
        dma((CHUNKS,)),
        dma((15,)),
        dma((6,)),
        dma((4,)),
    ]
    operands = (latent, w_in, output_weight, targets, area_weights.reshape(8, LANES))
    results = pl.pallas_call(
        kernel,
        out_shape=[
            V((8, LANES), F32),
            V(latent.shape, BF16),
            V((ROWS, FEATURES), F32),
            V((VARS, FEATURES), F32),
        ],
        in_specs=[pl.BlockSpec(memory_space=pltpu.HBM)] * 5 + [pl.BlockSpec(memory_space=pltpu.SMEM)],
        out_specs=[vmem] * 4,
        scratch_shapes=scratch,
        compiler_params=pltpu.CompilerParams(collective_id=1, has_side_effects=True, vmem_limit_bytes=48 << 20),
        name="energy_step",
    )(*[pltpu.with_memory_space_constraint(a, pltpu.HBM) for a in operands], live_counts)
    loss, glat, gwin, gwout = pl.pallas_call(
        write_out,
        out_shape=[
            jax.ShapeDtypeStruct((1, 1), F32),
            jax.ShapeDtypeStruct(latent.shape, BF16),
            jax.ShapeDtypeStruct((ROWS, FEATURES), F32),
            jax.ShapeDtypeStruct((VARS, FEATURES), F32),
        ],
        in_specs=[vmem] * 4,
        out_specs=[vmem] + [hbm] * 3,
        scratch_shapes=[dma((3,))],
        compiler_params=pltpu.CompilerParams(vmem_limit_bytes=1 << 20),
        name="write_out",
    )(*[pltpu.with_memory_space_constraint(r, pltpu.VMEM) for r in results])
    return loss.reshape(()), glat, gwin, gwout


def solution(mesh):
    placed = (P("ens", "sp", None), P(), P(), P(None, "sp"), P("sp"), P("sp"))
    return jax.shard_map(
        per_device,
        mesh=mesh,
        in_specs=placed,
        out_specs=(P(), P("ens", "sp", None), P("sp", None), P()),
        check_vma=False,
    )
```

```python
import functools
import math

import jax
import jax.numpy as jnp
from jax import lax
from jax.experimental import pallas as pl
from jax.experimental.pallas import tpu as pltpu
from jax.sharding import PartitionSpec as P

BF16, F32 = jnp.bfloat16, jnp.float32
MESH = pl.DeviceIdType.MESH
LOSS_SCALE = 1024.0
MEMBERS, VARS, FEATURES, POINTS = 8, 80, 1024, 1024
CHUNKS = 2
CHUNK = POINTS // CHUNKS
LANES = 128
HALF = FEATURES // 2
PIECES = ((0, 256, 128, "y"), (0, 384, 128, "z"), (1, 0, 256, "y"), (1, 256, 256, "z"))
SENDS = 8
FAR = ((2, 2), (2, 1), (2, 3), (1, 2), (3, 2))
ROWS = 32
OUTER = math.sqrt(2.0 / math.pi)
INNER = OUTER * 0.044715


def dot(a, b, ca, cb):
    return lax.dot_general(a, b, (((ca,), (cb,)), ((), ())), preferred_element_type=F32)


def activation(z):
    cubic = INNER * (z * z)
    t = jnp.tanh(z * (cubic + OUTER))
    h = z * (0.5 * t + 0.5)
    slope = (1.0 + t) * (1.0 + (1.0 - t) * (z * (3.0 * cubic + OUTER)))
    return h.astype(BF16), slope.astype(BF16)


def activation_only(z):
    return (z * (0.5 * jnp.tanh(z * (INNER * (z * z) + OUTER)) + 0.5)).astype(BF16)


def score_block(x_ref, y, weighted, store):
    n = MEMBERS
    pairs = [(i, j) for i in range(n) for j in range(i + 1, n)]
    step = 16
    own = [jnp.zeros((step, LANES), F32) for _ in range(n)]
    between = [jnp.zeros((step, LANES), F32) for _ in pairs]
    for v in range(0, VARS, step):
        x = [x_ref[m // 2, m % 2, v : v + step, :].astype(F32) for m in range(n)]
        for m in range(n):
            d = x[m] - y[v : v + step]
            own[m] = own[m] + d * d
        for q, (i, j) in enumerate(pairs):
            d = x[i] - x[j]
            between[q] = between[q] + d * d
    a = [jnp.sqrt(jnp.sum(o, axis=0, keepdims=True) + 1.0) for o in own]
    b = [jnp.sqrt(jnp.sum(o, axis=0, keepdims=True) + 1.0) for o in between]
    score = sum(a) / n - sum(b) / (n * (n - 1.0))
    from_target = [weighted / (n * t) for t in a]
    from_pair = [weighted / (n * (n - 1.0) * t) for t in b]
    for v in range(0, VARS, step):
        x = [x_ref[m // 2, m % 2, v : v + step, :].astype(F32) for m in range(n)]
        total = [(x[m] - y[v : v + step]) * from_target[m] for m in range(n)]
        for q, (i, j) in enumerate(pairs):
            d = (x[i] - x[j]) * from_pair[q]
            total[i] = total[i] - d
            total[j] = total[j] + d
        for m in range(n):
            store(m, v, step, total[m].astype(BF16))
    return weighted * score


def kernel(
    lat_hbm, w_hbm, wout_hbm, targets_hbm, area_hbm, live,
    loss_out, glat_out, gwin_out, gwout_out,
    lat, later, w, wout, targets, area, hid, back, acc, fsend, frecv, ssend, srecv, gout,
    core_send, core_recv, one_send, one_recv, two_send, two_recv, three,
    x_send, x_recv, xy_send, xy_recv, xz_send, x_all,
    g_core_send, g_core_recv, g_one_send, g_one_recv, g_two, g_three, g_all,
    ls_core, ls_y, ls_z, ls_x,
    in_sem, out_sem, f_rs, s_rs, p_rs, g_rs, t_rs,
):
    e = lax.axis_index("ens")
    sp = lax.axis_index("sp")
    core = lax.rem(sp, 2)
    z = lax.rem(sp // 2, 4)
    y = sp // 8

    def turn(i, d):
        return lax.rem(i + d, 4)

    def device(x_, y_, z_, core_):
        return (x_, (y_ * 4 + z_) * 2 + core_)

    along = {
        "x": lambda d: device(turn(e, d), y, z, core),
        "y": lambda d: device(e, turn(y, d), z, core),
        "z": lambda d: device(e, y, turn(z, d), core),
    }
    place = {"x": e, "y": y, "z": z}
    sibling = device(e, y, z, 1 - core)

    def load(m, c):
        s = pl.ds(c * CHUNK, CHUNK)
        return pltpu.make_async_copy(lat_hbm.at[m, s], lat.at[m, s], in_sem.at[2 * c + m])

    loads = {(c, m): load(m, c) for c in range(CHUNKS) for m in range(2)}
    small = [
        pltpu.make_async_copy(src, dst, in_sem.at[8 + i])
        for i, (src, dst) in enumerate([(area_hbm, area), (wout_hbm, wout), (targets_hbm, targets)])
    ]
    loads[0, 0].start()
    load_w = []
    for i in range(2):
        cols = pl.ds(i * HALF, HALF)
        load_w.append(pltpu.make_async_copy(w_hbm.at[:, cols], w.at[:, cols], in_sem.at[4 + i]))
        load_w[i].start()
    for cp in small:
        cp.start()

    peers = [along[k](d) for k in "xyz" for d in (1, 2, 3)] + [sibling]
    peers += [device(turn(e, dx), y, turn(z, dz), core) for dx in (1, 2, 3) for dz in (1, 2, 3)]
    barrier = pltpu.get_barrier_semaphore()
    for p in peers:
        pl.semaphore_signal(barrier, inc=1, device_id=p, device_id_type=MESH)

    def remote(src, dst, ss, rs, to):
        return pltpu.make_async_remote_copy(
            src_ref=src, dst_ref=dst, send_sem=ss, recv_sem=rs, device_id=to, device_id_type=MESH
        )

    leaving = {}
    turns = [0]

    def send(copies, rs, whole, sent=None):
        k = turns[0] % SENDS
        turns[0] += 1
        if k in leaving:
            leaving.pop(k)()
        ss = out_sem.at[k]
        for src, dst, to in copies:
            remote(src, dst, ss, rs, to).start()
        sent = whole if sent is None else sent
        leaving[k] = lambda: remote(sent, sent, ss, rs, sibling).wait_send()
        return lambda: remote(whole, whole, ss, rs, sibling).wait_recv()

    def spread(axis, src, dst, rs, whole, sent=None, hops=(2, 1, 3)):
        own = place[axis]
        return send([(src(turn(own, d)), dst(d, own), along[axis](d)) for d in hops], rs, whole, sent)

    def share(axis, buf, rs):
        return spread(axis, lambda k: buf.at[place[axis]], lambda d, own: buf.at[own], rs, buf.at[pl.ds(0, 3)])

    def four(ref):
        return (ref[0].astype(F32) + ref[1].astype(F32)) + (ref[2].astype(F32) + ref[3].astype(F32))

    def received(own, ref):
        total = own.astype(F32)
        for d in range(3):
            total = total + ref[d].astype(F32)
        return total

    def sums_tile(scores):
        where = lax.broadcasted_iota(jnp.int32, (8, LANES), 0) * LANES + lax.broadcasted_iota(jnp.int32, (8, LANES), 1)
        is_live = (where < live[0]).astype(F32)
        row = lax.broadcasted_iota(jnp.int32, (8, LANES), 0)
        weights = jnp.sum(area[...] * is_live, axis=0, keepdims=True)
        return jnp.where(row == 0, scores, jnp.where(row == 1, weights, jnp.sum(is_live, axis=0, keepdims=True)))

    def slopes_of_gelu(c, m):
        s = pl.ds(c * CHUNK, CHUNK)
        back[m, s, :] = activation(later[m, s, :])[1]

    def forecast(c, m):
        f = dot(wout[...], hid[m, c * CHUNK : (c + 1) * CHUNK, :], 1, 1).astype(BF16)
        for k in range(4):
            fsend[c, k, m] = f[:, k * LANES : (k + 1) * LANES]
        frecv[c, e, m] = fsend[c, e, m]

    def forward(c, m):
        s = pl.ds(c * CHUNK, CHUNK)
        pre = jnp.dot(lat[m, s, :], w[...], preferred_element_type=F32)
        hid[m, s, :] = activation_only(pre)
        later[m, s, :] = pre
        forecast(c, m)

    def forward_first(cols):
        pre = jnp.dot(lat[0, :CHUNK, :], w[:, cols], preferred_element_type=F32)
        hid[0, :CHUNK, cols], back[0, :CHUNK, cols] = activation(pre)

    def forward_send(c, m, hops=(2, 1, 3)):
        return spread(
            "x", lambda k: fsend.at[c, k, m], lambda d, own: frecv.at[c, own, m], f_rs.at[c, m],
            frecv.at[c, pl.ds(0, 3), m], frecv.at[c, pl.ds(0, len(hops)), m], hops,
        )

    def forward_half(c, m, hops):
        rows = [pl.ds(pl.multiple_of(c * CHUNK + turn(e, d) * LANES, LANES), LANES) for d in hops]
        pre = jnp.dot(
            jnp.concatenate([lat[m, r, :] for r in rows], axis=0), w[...], preferred_element_type=F32
        )
        h = activation_only(pre)
        for i, r in enumerate(rows):
            hid[m, r, :] = h[i * LANES : (i + 1) * LANES]
            later[m, r, :] = pre[i * LANES : (i + 1) * LANES]
        f = dot(wout[...], h, 1, 1).astype(BF16)
        for i, d in enumerate(hops):
            fsend[c, turn(e, d), m] = f[:, i * LANES : (i + 1) * LANES]

    def scored(c):
        block = c * 4 + e
        y_block = targets[:, pl.ds(pl.multiple_of(block * LANES, LANES), LANES)].astype(F32)
        lanes = lax.broadcasted_iota(jnp.int32, (1, LANES), 1)
        weighted = area[pl.ds(block, 1), :] * (block * LANES + lanes < live[0]).astype(F32)

        def store(m, v, step, value):
            ssend[c, m // 2, m % 2, v : v + step, :] = value

        row = score_block(frecv.at[c], y_block, weighted, store)
        srecv[c, e] = ssend[c, e]
        return row

    def scored_send(c):
        return spread(
            "x", lambda k: ssend.at[c, k], lambda d, own: srecv.at[c, own], s_rs.at[c], srecv.at[c, pl.ds(0, 3)]
        )

    def backward(c, lo, wide):
        s, cols = pl.ds(c * CHUNK, CHUNK), slice(lo, lo + wide)
        for m in range(2):
            slopes = jnp.concatenate([srecv[c, k, m] for k in range(4)], axis=1)
            bh = dot(slopes, wout[:, cols], 0, 0)
            back[m, s, cols] = (back[m, s, cols].astype(F32) * bh).astype(BF16)

    def output_part(c):
        s = pl.ds(c * CHUNK, CHUNK)
        slopes = jnp.concatenate([srecv[c, k, m] for m in range(2) for k in range(4)], axis=1)
        term = dot(slopes, hid[:, s, :].reshape(2 * CHUNK, FEATURES), 1, 0)
        if c == 0:
            gout[...] = term
        else:
            gout[...] += term

    def weight_early():
        a = lat[:, :CHUNK, :].reshape(2 * CHUNK, FEATURES)
        term = dot(a, back[:, :CHUNK, :].reshape(2 * CHUNK, FEATURES), 0, 0)
        for i in range(2):
            acc[i] = term[:, i * HALF : (i + 1) * HALF].reshape(16, 2, ROWS, HALF)

    def weight_half(i):
        cols = slice(i * HALF, (i + 1) * HALF)
        a = lat[:, CHUNK:, :].reshape(2 * CHUNK, FEATURES)
        acc[i] += dot(a, back[:, CHUNK:, cols].reshape(2 * CHUNK, HALF), 0, 0).reshape(16, 2, ROWS, HALF)

    def g_start():
        def body(k, _):
            cols = pl.ds(pl.multiple_of((k * 2 + 1 - core) * LANES, LANES), LANES)
            g_core_send[k] = gout[:, cols].astype(BF16)
            return 0

        lax.fori_loop(0, 4, body, 0)
        return send([(g_core_send, g_core_recv, sibling)], g_rs.at[0], g_core_recv)

    def g_to_first(arrived):
        arrived()

        def body(k, _):
            cols = pl.ds(pl.multiple_of((k * 2 + core) * LANES, LANES), LANES)
            g_one_send[k] = (gout[:, cols] + g_core_recv[k].astype(F32)).astype(BF16)
            return 0

        lax.fori_loop(0, 4, body, 0)
        return spread("y", lambda k: g_one_send.at[k], lambda d, own: g_one_recv.at[d - 1], g_rs.at[1], g_one_recv)

    def g_to_second(arrived):
        arrived()
        g_two[e] = received(g_one_send[y], g_one_recv).astype(BF16)
        return share("x", g_two, g_rs.at[2])

    def g_to_third(arrived):
        arrived()
        g_three[z] = four(g_two).astype(BF16)
        return share("z", g_three, g_rs.at[3])

    def g_to_all(arrived, share_of):
        arrived()
        g_all[core, y] = (four(g_three) * share_of).astype(BF16)
        return spread("y", lambda k: g_all.at[core, y], lambda d, own: g_all.at[core, own], g_rs.at[4], g_all.at[0, pl.ds(0, 3)])

    def g_to_sibling(arrived):
        arrived()
        return send([(g_all.at[core], g_all.at[core], sibling)], g_rs.at[5], g_all.at[0])

    def g_finish(arrived):
        arrived()
        for k in range(8):
            gwout_out[:, k * LANES : (k + 1) * LANES] = g_all[k % 2, k // 2].astype(F32)

    def to_core(i):
        core_send[i] = acc[i, :, 1 - core].astype(BF16)
        return send([(core_send.at[i], core_recv.at[i], sibling)], p_rs.at[i], core_recv.at[i])

    def from_core(i, lo, wide):
        cols = slice(lo, lo + wide)
        return (acc[i, :, core, :, cols] + core_recv[i, :, :, cols].astype(F32)).astype(BF16)

    def part(j, k):
        return one_send[j].at[k] if PIECES[j][3] == "y" else one_send[j].at[:, k]

    def to_first(j):
        half, lo, wide, axis = PIECES[j]
        one_send[j][...] = from_core(half, lo, wide).reshape(4, 4, ROWS, wide)
        return spread(
            axis, lambda k: part(j, k), lambda d, own: one_recv[j].at[d - 1], p_rs.at[2 + j], one_recv[j]
        )

    def to_second(j, arrived):
        arrived()
        axis = PIECES[j][3]
        two_send[j][...] = received(part(j, place[axis])[...], one_recv[j]).astype(BF16)
        return spread(
            "z" if axis == "y" else "y", lambda k: two_send[j].at[k], lambda d, own: two_recv[j].at[d - 1],
            p_rs.at[6 + j], two_recv[j],
        )

    def to_third(i, arrived):
        for j in (2 * i, 2 * i + 1):
            arrived[j]()
            wide, own = PIECES[j][2], place["z" if PIECES[j][3] == "y" else "y"]
            lo = (j % 2) * wide
            three[i][e, :, lo : lo + wide] = received(two_send[j][own], two_recv[j]).astype(BF16)
        return share("x", three[i], p_rs.at[10 + i])

    def finish(i, arrived, share_of):
        arrived()
        wide = 2 * PIECES[2 * i][2]
        gwin_out[:, FEATURES // 4 * (1 + i) : FEATURES // 4 * (1 + i) + wide] = four(three[i]) * share_of

    def x_block(k):
        return slice((k // 2) * 16, (k // 2 + 1) * 16), slice((k % 2) * LANES, (k % 2 + 1) * LANES)

    def x_first():
        total = from_core(0, 0, 2 * LANES)
        for k in range(4):
            rows, cols = x_block(k)
            x_send[k] = total[:, rows, cols]
        return spread("x", lambda k: x_send.at[k], lambda d, own: x_recv.at[d - 1], p_rs.at[12], x_recv)

    def x_second(arrived):
        arrived()
        xy_send[...] = received(x_send[e], x_recv).astype(BF16).reshape(4, 4, 16, LANES)
        return spread("y", lambda k: xy_send.at[k], lambda d, own: xy_recv.at[d - 1], p_rs.at[13], xy_recv)

    def x_third(arrived):
        arrived()
        xz_send[...] = received(xy_send[y], xy_recv).astype(BF16)
        slot = e * 4 + z
        x_all[slot] = xz_send[z]
        copies = []
        for dx, dz in sorted(((i, j) for i in range(4) for j in range(4) if i or j), key=lambda h: h not in FAR):
            to = turn(z, dz)
            copies.append((xz_send.at[to], x_all.at[slot], device(turn(e, dx), y, to, core)))
        return send(copies, p_rs.at[14], x_all.at[pl.ds(0, 15)])

    def x_finish(arrived, share_of):
        arrived()
        for k in range(4):
            rows, cols = x_block(k)
            gwin_out[rows, cols] = four(x_all.at[pl.ds(4 * k, 4)]) * share_of

    def latent_tile(i, factor):
        m, s = i // 2, pl.ds((i % 2) * CHUNK, CHUNK)
        glat_out[m, s, :] = (dot(back[m, s, :], w[...], 1, 1) * factor).astype(BF16)

    def block(run, *args):
        pl.when(core < 2)(lambda: run(*args))

    loads[0, 0].wait()
    load_w[0].wait()
    loads[0, 1].start()
    for i in range(2):
        cols = slice(i * HALF, (i + 1) * HALF)
        if i == 1:
            load_w[1].wait()
            loads[1, 0].start()
            loads[1, 1].start()
        block(forward_first, cols)
    small[1].wait()
    block(forecast, 0, 0)
    pl.semaphore_wait(barrier, len(peers))
    f00 = forward_send(0, 0)
    loads[0, 1].wait()
    block(forward, 0, 1)
    f01 = forward_send(0, 1)
    loads[1, 0].wait()
    block(forward, 1, 0)
    f10 = forward_send(1, 0)
    loads[1, 1].wait()
    block(forward_half, 1, 1, (2, 1))
    f11 = forward_send(1, 1, (2, 1))
    f00()
    f01()
    small[0].wait()
    small[2].wait()
    row0 = scored(0)
    s0 = scored_send(0)
    block(forward_half, 1, 1, (3, 0))
    forward_send(1, 1, (3,))
    frecv[1, e, 1] = fsend[1, e, 1]
    block(slopes_of_gelu, 0, 1)
    block(slopes_of_gelu, 1, 0)
    block(slopes_of_gelu, 1, 1)
    f10()
    f11()
    row1 = scored(1)
    s1 = scored_send(1)
    ls_core[core] = sums_tile(row0 + row1)
    lc = send([(ls_core.at[core], ls_core.at[core], sibling)], t_rs.at[0], ls_core.at[0])
    s0()
    block(backward, 0, 0, FEATURES)
    block(output_part, 0)
    lc()
    ls_y[y] = ls_core[0] + ls_core[1]
    lc = share("y", ls_y, t_rs.at[1])
    block(weight_early)
    s1()
    block(output_part, 1)
    g = g_start()
    lc()
    ls_z[z] = four(ls_y)
    lc = share("z", ls_z, t_rs.at[2])
    block(backward, 1, 0, HALF)
    block(weight_half, 0)
    c0 = to_core(0)
    g = g_to_first(g)
    block(backward, 1, HALF, HALF)
    block(weight_half, 1)
    c1 = to_core(1)
    c0()
    p = {}
    xf = x_first()
    p[0] = to_first(0)
    p[1] = to_first(1)
    lc()
    sums = four(ls_z)
    ls_x[e] = sums
    lc = share("x", ls_x, t_rs.at[3])
    totals = jnp.sum(sums, axis=1, keepdims=True)
    weight_total, live_total = totals[1:2, 0:1], totals[2:3, 0:1]
    factor = 0.5 * LOSS_SCALE * live_total / weight_total
    c1()
    p[2] = to_first(2)
    p[3] = to_first(3)
    block(latent_tile, 0, factor)
    g = g_to_second(g)
    block(latent_tile, 1, factor)
    block(latent_tile, 2, factor)
    xf = x_second(xf)
    p[0] = to_second(0, p[0])
    p[1] = to_second(1, p[1])
    g = g_to_third(g)
    block(latent_tile, 3, factor)
    lc()
    loss_out[...] = jnp.sum(four(ls_x), axis=1, keepdims=True) / weight_total + jnp.zeros((8, LANES), F32)
    share_of = LOSS_SCALE / weight_total
    half_share = 0.5 * share_of
    p[2] = to_second(2, p[2])
    p[3] = to_second(3, p[3])
    xf = x_third(xf)
    xa = to_third(0, p)
    g = g_to_all(g, share_of)
    xb = to_third(1, p)
    finish(0, xa, half_share)
    g = g_to_sibling(g)
    x_finish(xf, half_share)
    g_finish(g)
    finish(1, xb, half_share)
    for left in leaving.values():
        left()


def write_out(loss, glat, gwin, gwout, loss_out, glat_out, gwin_out, gwout_out, sem):
    pairs = [(glat, glat_out), (gwin, gwin_out), (gwout, gwout_out)]
    cps = [pltpu.make_async_copy(src, dst, sem.at[i]) for i, (src, dst) in enumerate(pairs)]
    for cp in cps:
        cp.start()
    loss_out[...] = loss[0:1, 0:1]
    for cp in cps:
        cp.wait()


def per_device(latent, w_in, output_weight, targets, area_weights, live_counts):
    vmem = pl.BlockSpec(memory_space=pltpu.VMEM)
    hbm = pl.BlockSpec(memory_space=pl.ANY)
    V = pltpu.VMEM
    dma = pltpu.SemaphoreType.DMA
    widths = [p[2] for p in PIECES]
    scratch = [
        V((2, POINTS, FEATURES), BF16),
        V((2, POINTS, FEATURES), F32),
        V((FEATURES, FEATURES), BF16),
        V((VARS, FEATURES), BF16),
        V((VARS, POINTS), BF16),
        V((8, LANES), F32),
        V((2, POINTS, FEATURES), BF16),
        V((2, POINTS, FEATURES), BF16),
        V((2, 16, 2, ROWS, HALF), F32),
        V((CHUNKS, 4, 2, VARS, LANES), BF16),
        V((CHUNKS, 4, 2, VARS, LANES), BF16),
        V((CHUNKS, 4, 2, VARS, LANES), BF16),
        V((CHUNKS, 4, 2, VARS, LANES), BF16),
        V((VARS, FEATURES), F32),
        V((2, 16, ROWS, HALF), BF16),
        V((2, 16, ROWS, HALF), BF16),
        [V((4, 4, ROWS, n), BF16) for n in widths],
        [V((3, 4, ROWS, n), BF16) for n in widths],
        [V((4, ROWS, n), BF16) for n in widths],
        [V((3, ROWS, n), BF16) for n in widths],
        [V((4, ROWS, 2 * widths[0]), BF16), V((4, ROWS, 2 * widths[2]), BF16)],
        V((4, 16, 16, LANES), BF16),
        V((3, 16, 16, LANES), BF16),
        V((4, 4, 16, LANES), BF16),
        V((3, 4, 16, LANES), BF16),
        V((4, 16, LANES), BF16),
        V((16, 16, LANES), BF16),
        V((4, VARS, LANES), BF16),
        V((4, VARS, LANES), BF16),
        V((4, VARS, LANES), BF16),
        V((3, VARS, LANES), BF16),
        V((4, VARS, LANES), BF16),
        V((4, VARS, LANES), BF16),
        V((2, 4, VARS, LANES), BF16),
        V((2, 8, LANES), F32),
        V((4, 8, LANES), F32),
        V((4, 8, LANES), F32),
        V((4, 8, LANES), F32),
        dma((11,)),
        dma((SENDS,)),
        dma((CHUNKS, 2)),
        dma((CHUNKS,)),
        dma((15,)),
        dma((6,)),
        dma((4,)),
    ]
    operands = (latent, w_in, output_weight, targets, area_weights.reshape(8, LANES))
    results = pl.pallas_call(
        kernel,
        out_shape=[
            V((8, LANES), F32),
            V(latent.shape, BF16),
            V((ROWS, FEATURES), F32),
            V((VARS, FEATURES), F32),
        ],
        in_specs=[pl.BlockSpec(memory_space=pltpu.HBM)] * 5 + [pl.BlockSpec(memory_space=pltpu.SMEM)],
        out_specs=[vmem] * 4,
        scratch_shapes=scratch,
        compiler_params=pltpu.CompilerParams(collective_id=1, has_side_effects=True, vmem_limit_bytes=48 << 20),
        name="energy_step",
    )(*[pltpu.with_memory_space_constraint(a, pltpu.HBM) for a in operands], live_counts)
    loss, glat, gwin, gwout = pl.pallas_call(
        write_out,
        out_shape=[
            jax.ShapeDtypeStruct((1, 1), F32),
            jax.ShapeDtypeStruct(latent.shape, BF16),
            jax.ShapeDtypeStruct((ROWS, FEATURES), F32),
            jax.ShapeDtypeStruct((VARS, FEATURES), F32),
        ],
        in_specs=[vmem] * 4,
        out_specs=[vmem] + [hbm] * 3,
        scratch_shapes=[dma((3,))],
        compiler_params=pltpu.CompilerParams(vmem_limit_bytes=1 << 20),
        name="write_out",
    )(*[pltpu.with_memory_space_constraint(r, pltpu.VMEM) for r in results])
    return loss.reshape(()), glat, gwin, gwout


def solution(mesh):
    placed = (P("ens", "sp", None), P(), P(), P(None, "sp"), P("sp"), P("sp"))
    return jax.shard_map(
        per_device,
        mesh=mesh,
        in_specs=placed,
        out_specs=(P(), P("ens", "sp", None), P("sp", None), P()),
        check_vma=False,
    )
```
